128 devices in a mesh: ab: 8 (over y_lo, z), cd: 16 (over x, y_hi, core).
Axes of the slice: x: 4, y: 4 (y_hi: 2, y_lo: 2; y = y_hi * 2 + y_lo), z: 4, core: 2. Of those that a mesh axis runs over, the one named last changes fastest.
Arguments:
- amplitudes: bfloat16 [1024, 51200], P('ab', 'cd'), may hold values from -6 to 6
- integrals: bfloat16 [16384, 51200], P('ab', 'cd'), may hold values from -0.078125 to 0.078125
- ab_sizes: int32 [8], replicated, may hold values from 1 to 4096, 16384 in all
- cd_sizes: int32 [8], replicated, may hold values from 1 to 12800, 51200 in all
- pair_index: int32 [1024], replicated, may hold values from 0 to 1023, each once
Outputs:
- ladder: float32 [1024, 16384], P(None, ('ab', 'cd'))
The draws below stay inside these ranges and needn't reach their ends.
Inputs may be any that keep to these rules, and one draw needn't show every extreme that they name: `ab_sizes`: block sizes are positive and sum to 16384, the largest is exactly 4096. `cd_sizes`: block sizes are positive and sum to 51200, the largest is exactly 12800. `pair_index`: each residual row once.
All inputs are finite; a program needn't handle non-finite values.
Results may differ from the reference program's by a relative error of at most 0.0003.
Values may be sent and summed in bfloat16 or wider, within the bound.
A program may use at most 128 MiB of HBM per device.

```python
import math
import jax
import jax.numpy as jnp
import numpy as np
from jax import lax

NIRREP = 8
AB_DEV = 2048
AB = 16384
CD = 51200
OCCP = 1024
N_AB = 8


def level_of(rng, shape, cuts, smallest, largest):
    def one(position, blocks):
        steps = jax.random.uniform(jax.random.fold_in(jax.random.fold_in(rng, 6), position), (blocks,), jnp.float32, smallest / len(cuts), largest / len(cuts))
        return jnp.repeat(jnp.exp(steps), shape[position] // blocks).reshape((-1,) + (1,) * (len(shape) - position - 1))

    loudness = one(*cuts[0])
    for cut in cuts[1:]:
        loudness = loudness * one(*cut)
    return loudness


def split_up(number_of, total, limit, slope):
    loads = [(1 << 20) // math.isqrt(rank ** slope) + 1 for rank in range(2, number_of + 1)]
    surplus, given = total - limit - (number_of - 1), [1] * (number_of - 1)
    while surplus > 0:
        candidates = [i for i in range(number_of - 1) if given[i] < limit]
        mass, remaining = sum([loads[i] for i in candidates]), surplus
        for i in candidates:
            more = min(limit - given[i], max(1, remaining * loads[i] // mass), surplus)
            given[i] = given[i] + more
            surplus = surplus - more
    return np.array([limit] + given)


def ragged(own_key, number_of, total, reach, slope):
    if number_of == 2:
        one = jax.random.randint(own_key, (), max(1, total - reach), min(reach, total - 1) + 1)
        return jnp.stack([one, total - one])
    lengths = jnp.asarray(split_up(number_of, total, reach, slope), jnp.int32)
    twos = (number_of - 1) // 2
    giver, receiver = lengths[1:1 + 2 * twos:2], lengths[2:2 + 2 * twos:2]
    slack = jnp.minimum(giver - 1, reach - receiver)
    shifted = jax.random.randint(jax.random.fold_in(own_key, 1), (twos,), 0, 1 << 20) % (slack + 1)
    lengths = lengths.at[1:1 + 2 * twos:2].set(giver - shifted).at[2:2 + 2 * twos:2].set(receiver + shifted)
    return lengths[jax.random.permutation(jax.random.fold_in(own_key, 2), number_of)]


def noise(stream_key, shape, width, bound, shards=(), kind=jnp.bfloat16):
    values = width * jax.random.normal(stream_key, shape, jnp.float32)
    if shards:
        values = values * level_of(stream_key, shape, shards, -0.22, 0.18)
    return jnp.clip(values, -bound, bound).astype(kind)


def setup_inputs(seed: int = 0) -> dict:
    keys = jax.random.split(jax.random.key(seed), 6)
    return {
        "amplitudes": noise(keys[0], (OCCP, CD), 1.0, 6.0, ((0, 8), (1, 16))),
        "integrals": noise(keys[1], (AB, CD), (CD // 8) ** -0.5, 0.078125, ((0, 8), (1, 16))),
        "ab_sizes": ragged(keys[2], NIRREP, AB, AB // 4, 2).astype(jnp.int32),
        "cd_sizes": ragged(keys[3], NIRREP, CD, CD // 4, 2).astype(jnp.int32),
        "pair_index": jax.random.permutation(keys[4], OCCP).astype(jnp.int32),
    }


def irrep_labels(sizes, start, count):
    ends = jnp.cumsum(sizes).astype(jnp.int32)
    where_at = start + jnp.arange(count, dtype=jnp.int32)
    return jnp.sum((where_at[:, None] >= ends[None, :]).astype(jnp.int32), axis=1)


def reference(amplitudes, integrals, ab_sizes, cd_sizes, pair_index):
    cd_label = irrep_labels(cd_sizes, 0, CD)
    blocks = integrals.reshape(N_AB, AB_DEV, CD)

    def one_block(args):
        slab, first = args
        ab_label = irrep_labels(ab_sizes, first, AB_DEV)
        masked = jnp.where(ab_label[:, None] == cd_label[None, :], slab, jnp.zeros_like(slab))
        return lax.dot_general(amplitudes, masked, (((1,), (1,)), ((), ())), preferred_element_type=jnp.float32)

    starts = (jnp.arange(N_AB, dtype=jnp.int32) * AB_DEV).astype(jnp.int32)
    parts = lax.map(one_block, (blocks, starts))
    product = jnp.transpose(parts, (1, 0, 2)).reshape(OCCP, AB)
    return jnp.zeros((OCCP, AB), jnp.float32).at[pair_index].set(product)
```

```python
import functools

import jax
import jax.numpy as jnp
from jax import lax
from jax.experimental import pallas as pl
from jax.experimental.pallas import tpu as pltpu
from jax.sharding import PartitionSpec as P

MESH = pl.DeviceIdType.MESH
BF16, F32, I32 = jnp.bfloat16, jnp.float32, jnp.int32

PANELS = 8
LANES = 128
CHUNK = 16
DX = (2, 1, 3, 0)
AHEAD = 1

CROSS = 8
CUT = 13
CUT_REST = 16

GROUPS = ((0, 1), (1, 1), (2, 2), (4, 2), (6, 1), (7, 1))
SLOTS = {
    1: (("T00", "T01"), ("T02", "T03")),
    2: (("T10", "T11"), ("R05", "T12", "T13")),
    3: (("R06",), ("R15",)),
    4: (("R16", "T20"), ("T21",)),
    5: (("T22",), ("T23",)),
    6: (("T30", "T31", "R25"), ("T32", "T33", "R26")),
    7: (("T40", "T41", "R35"), ("T42", "T43", "R36")),
}
TAIL = ("T50", "T51", "R45", "T52", "T53", "R46", "R55", "R56")


def kernel(
    ab_sizes, cd_sizes, pairs_ref, amps_ref, ints_ref, out_ref,
    amps, ints, prod, from_core, x_one, x_two, from_y, cd_lab,
    g_send, g_recv, r_send, r_recv, local_sem,
):
    panel_rows, depth = amps_ref.shape
    ab_rows = ints_ref.shape[0]
    rounds = panel_rows // CHUNK
    lane_tiles = depth // LANES
    round_rows = PANELS * CHUNK

    ab, cd = lax.axis_index("ab"), lax.axis_index("cd")
    yl, z = ab // 4, lax.rem(ab, 4)
    x, yh, core = cd // 4, lax.rem(cd // 2, 2), lax.rem(cd, 2)
    z_up, z_down, z_far = lax.rem(z + 1, 4), lax.rem(z + 3, 4), lax.rem(z + 2, 4)
    mine, other = yl * 4, (1 - yl) * 4

    to_pair = {"ab": other + z, "cd": cd}
    to_up = {"ab": mine + z_up, "cd": cd}
    to_down = {"ab": mine + z_down, "cd": cd}
    to_core = {"ab": ab, "cd": x * 4 + yh * 2 + (1 - core)}
    to_y = {"ab": ab, "cd": x * 4 + (1 - yh) * 2 + core}
    to_right = {"ab": ab, "cd": lax.rem(x + 1, 4) * 4 + yh * 2 + core}
    to_left = {"ab": ab, "cd": lax.rem(x + 3, 4) * 4 + yh * 2 + core}

    def ints_copy(block):
        dx, dc, dy = DX[block // 4], 1 - (block // 2) % 2, block % 2
        part = lax.rem(x + dx, 4) * 4 + (yh + dy - 2 * yh * dy) * 2 + (core + dc - 2 * core * dc)
        start = pl.multiple_of(part * LANES, LANES)
        copy = pltpu.make_async_copy(
            ints_ref.at[pl.ds(start, LANES), :],
            ints.at[pl.ds(block * LANES, LANES), :],
            local_sem.at[block],
        )
        return copy, start

    blocks = ab_rows // LANES
    for block in range(blocks):
        ints_copy(block)[0].start()

    barrier = pltpu.get_barrier_semaphore()
    neighbours = (to_pair, to_up, to_down, to_core, to_y, to_right, to_left)
    for neighbour in neighbours:
        pl.semaphore_signal(barrier, inc=1, device_id=neighbour, device_id_type=MESH)
    pl.semaphore_wait(barrier, len(neighbours))

    def slot(q, owner, low, high):
        start = pl.multiple_of(q * round_rows + owner * CHUNK, CHUNK)
        return amps.at[pl.ds(start, CHUNK), pl.ds(low * LANES, (high - low) * LANES)]

    full, cross, rest = (0, lane_tiles), (0, CROSS), (CROSS, lane_tiles)
    low_cut, high_cut = (0, CUT), (CUT, lane_tiles)
    low_rest, high_rest = (CROSS, CUT_REST), (CUT_REST, lane_tiles)
    me, up, down, far = mine + z, mine + z_up, mine + z_down, mine + z_far
    o_me, o_up, o_down, o_far = other + z, other + z_up, other + z_down, other + z_far
    kinds = (
        (me, full, to_pair, o_me),
        (me, full, to_up, down),
        (me, full, to_down, up),
        (o_me, rest, to_up, o_down),
        (o_me, rest, to_down, o_up),
        (down, low_cut, to_up, far),
        (up, high_cut, to_down, far),
        (down, cross, to_pair, o_down),
        (up, cross, to_pair, o_up),
        (o_down, low_rest, to_up, o_far),
        (o_up, high_rest, to_down, o_far),
        (far, cross, to_pair, o_far),
    )

    def g_out(q, kind):
        owner, columns, target, _ = kinds[kind]
        ref = slot(q, owner, *columns)
        return pltpu.make_async_remote_copy(
            src_ref=ref, dst_ref=ref, send_sem=g_send.at[kind, q], recv_sem=g_recv.at[kind, q],
            device_id=target, device_id_type=MESH,
        )

    def g_in(q, kind):
        _, columns, target, owner = kinds[kind]
        ref = slot(q, owner, *columns)
        return pltpu.make_async_remote_copy(
            src_ref=ref, dst_ref=ref, send_sem=g_send.at[kind, q], recv_sem=g_recv.at[kind, q],
            device_id=target, device_id_type=MESH,
        )

    def first(q):
        if q < rounds:
            for kind in (1, 2, 0):
                g_out(q, kind).start()

    def second(q):
        g_in(q, 1).wait_recv()
        g_out(q, 5).start()
        g_out(q, 7).start()
        g_in(q, 2).wait_recv()
        g_out(q, 6).start()
        g_out(q, 8).start()
        g_in(q, 0).wait_recv()
        g_out(q, 3).start()
        g_out(q, 4).start()

    def third(q):
        g_in(q, 5).wait_recv()
        g_out(q, 11).start()
        g_in(q, 3).wait_recv()
        g_out(q, 9).start()
        g_in(q, 4).wait_recv()
        g_out(q, 10).start()

    def arrived(q):
        for kind in (6, 7, 8, 9, 10, 11):
            g_in(q, kind).wait_recv()

    for q in range(rounds):
        amps[pl.ds(pl.multiple_of(q * round_rows + me * CHUNK, CHUNK), CHUNK), :] = (
            amps_ref[pl.ds(q * CHUNK, CHUNK), :]
        )
    for q in range(1 + AHEAD):
        first(q)

    def ends(sizes):
        out, total = [], jnp.int32(0)
        for k in range(sizes.shape[0]):
            total = total + sizes[k]
            out.append(total)
        return out

    def labels(where_at, limits):
        label = jnp.zeros(where_at.shape, I32)
        for limit in limits:
            label = label + (where_at >= limit).astype(I32)
        return label.astype(F32).astype(BF16)

    ab_ends, cd_ends = ends(ab_sizes), ends(cd_sizes)
    cd_lab[...] = labels(cd * depth + lax.broadcasted_iota(I32, cd_lab.shape, 1), cd_ends)

    def mask(block):
        copy, start = ints_copy(block)
        copy.wait()
        at = lax.broadcasted_iota(I32, (LANES, LANES), 0) + (ab * ab_rows + start)
        ab_lab = labels(at, ab_ends)

        def one(k, carry):
            columns = pl.ds(pl.multiple_of(k * LANES, LANES), LANES)
            rows = pl.ds(block * LANES, LANES)
            here = jnp.broadcast_to(cd_lab[0:1, columns], (LANES, LANES))
            tile = ints[rows, columns]
            ints[rows, columns] = jnp.where(ab_lab == here, tile, jnp.zeros_like(tile))
            return carry

        lax.fori_loop(0, lane_tiles, one, 0)

    wide = 4 * LANES
    half = 2 * LANES

    def r_copy(g, kind, src, dst, target):
        return pltpu.make_async_remote_copy(
            src_ref=src, dst_ref=dst, send_sem=r_send.at[kind, g], recv_sem=r_recv.at[kind, g],
            device_id=target, device_id_type=MESH,
        )

    def rows_of(g):
        begin, count = GROUPS[g]
        return pl.ds(begin * round_rows, count * round_rows)

    def core_copy(g, k):
        rows = rows_of(g)
        return r_copy(
            g, k, prod.at[rows, pl.ds(k * wide, half)], from_core.at[rows, pl.ds(k * half, half)], to_core
        )

    def x_one_copy(g, way):
        rows = rows_of(g)
        return r_copy(
            g, 4 + way, prod.at[rows, pl.ds(half + way * LANES, LANES)], x_one.at[way, rows, :],
            (to_right, to_left)[way],
        )

    def x_two_copy(g, way):
        rows = rows_of(g)
        return r_copy(
            g, 6 + way, prod.at[rows, pl.ds((1 + way) * wide + half, half)], x_two.at[way, rows, :],
            (to_right, to_left)[way],
        )

    def y_copy(g):
        rows = rows_of(g)
        return r_copy(g, 8, prod.at[rows, pl.ds(3 * wide + half + LANES, LANES)], from_y.at[rows, :], to_y)

    def kept(k):
        return pl.ds(k * wide + half, half)

    def tile(g, k):
        rows = rows_of(g)
        prod[rows, pl.ds(k * wide, wide)] = lax.dot_general(
            amps[rows, :], ints[pl.ds(k * wide, wide), :], (((1,), (1,)), ((), ())),
            preferred_element_type=F32,
        )
        core_copy(g, k).start()
        if k == 1:
            core_copy(g, 0).wait_recv()
            prod[rows, kept(0)] += from_core[rows, pl.ds(0, half)]
            x_one_copy(g, 0).start()
            x_one_copy(g, 1).start()
        if k == 3:
            for way in range(2):
                core_copy(g, 1 + way).wait_recv()
                prod[rows, kept(1 + way)] += from_core[rows, pl.ds((1 + way) * half, half)]
                x_one_copy(g, way).wait_recv()
                prod[rows, pl.ds((1 + way) * wide + half + way * LANES, LANES)] += x_one[way, rows, :]
                x_two_copy(g, way).start()

    def sum_x(g):
        rows = rows_of(g)
        core_copy(g, 3).wait_recv()
        total = prod[rows, kept(3)] + from_core[rows, pl.ds(3 * half, half)]
        x_two_copy(g, 0).wait_recv()
        x_two_copy(g, 1).wait_recv()
        prod[rows, kept(3)] = total + x_two[0, rows, :] + x_two[1, rows, :]
        y_copy(g).start()

    def place(g):
        begin, count = GROUPS[g]
        y_copy(g).wait_recv()
        for q in range(begin, begin + count):
            rows = pl.ds(q * round_rows, round_rows)
            found = prod[rows, pl.ds(3 * wide + half, LANES)] + from_y[rows, :]
            high = found.astype(BF16)
            left = found - high.astype(F32)
            mid = left.astype(BF16)
            low = (left - mid.astype(F32)).astype(BF16)
            target = jnp.broadcast_to(pairs_ref[pl.ds(q, 1), :], out_ref.shape)
            goes = lax.broadcasted_iota(I32, out_ref.shape, 0) == target
            goes = jnp.where(goes, 1.0, 0.0).astype(BF16)
            term = jnp.dot(
                jnp.concatenate([goes, goes, goes], axis=1),
                jnp.concatenate([high, mid, low], axis=0),
                preferred_element_type=F32,
            )
            if q == 0:
                out_ref[...] = term
            else:
                out_ref[...] += term

    def run(steps):
        for step in steps:
            g, k = int(step[1]), int(step[2])
            if step[0] == "T":
                tile(g, k)
            elif k == 5:
                sum_x(g)
            else:
                place(g)

    for block in range(blocks // 2):
        mask(block)
    second(0)
    first(1 + AHEAD)
    for block in range(blocks // 2, blocks):
        mask(block)
    third(0)
    arrived(0)
    for q in range(1, rounds):
        second(q)
        first(q + 1 + AHEAD)
        run(SLOTS[q][0])
        third(q)
        run(SLOTS[q][1])
        arrived(q)
    run(TAIL)

    for q in range(rounds):
        for kind in range(len(kinds)):
            g_out(q, kind).wait_send()
    for g in range(len(GROUPS)):
        for k in range(4):
            core_copy(g, k).wait_send()
        for way in range(2):
            x_one_copy(g, way).wait_send()
            x_two_copy(g, way).wait_send()
        y_copy(g).wait_send()


def shards(amplitudes, integrals, ab_sizes, cd_sizes, pair_index):
    panel_rows, depth = amplitudes.shape
    ab_rows = integrals.shape[0]
    all_pairs = pair_index.shape[0]
    rounds = panel_rows // CHUNK
    keeps = ab_rows // lax.axis_size("cd")
    pairs = pair_index.reshape(PANELS, rounds, CHUNK).transpose(1, 0, 2).reshape(rounds, PANELS * CHUNK)
    vmem, smem = pl.BlockSpec(memory_space=pltpu.VMEM), pl.BlockSpec(memory_space=pltpu.SMEM)
    return pl.pallas_call(
        kernel,
        out_shape=jax.ShapeDtypeStruct((all_pairs, keeps), F32),
        in_specs=[smem, smem, vmem, vmem, pl.BlockSpec(memory_space=pl.ANY)],
        out_specs=vmem,
        scratch_shapes=[
            pltpu.VMEM((all_pairs, depth), BF16),
            pltpu.VMEM((ab_rows, depth), BF16),
            pltpu.VMEM((all_pairs, ab_rows), F32),
            pltpu.VMEM((all_pairs, ab_rows // 2), F32),
            pltpu.VMEM((2, all_pairs, keeps), F32),
            pltpu.VMEM((2, all_pairs, 2 * keeps), F32),
            pltpu.VMEM((all_pairs, keeps), F32),
            pltpu.VMEM((16, depth), BF16),
            pltpu.SemaphoreType.DMA((12, rounds)),
            pltpu.SemaphoreType.DMA((12, rounds)),
            pltpu.SemaphoreType.DMA((9, len(GROUPS))),
            pltpu.SemaphoreType.DMA((9, len(GROUPS))),
            pltpu.SemaphoreType.DMA((ab_rows // LANES,)),
        ],
        name="ladder",
        compiler_params=pltpu.CompilerParams(
            collective_id=0, has_side_effects=True, vmem_limit_bytes=56 << 20
        ),
    )(ab_sizes, cd_sizes, pairs, amplitudes, integrals)


def solution(mesh):
    return jax.shard_map(
        shards,
        mesh=mesh,
        in_specs=(P("ab", "cd"), P("ab", "cd"), P(), P(), P()),
        out_specs=P(None, ("ab", "cd")),
        check_vma=False,
    )
```

```python
import functools

import jax
import jax.numpy as jnp
from jax import lax
from jax.experimental import pallas as pl
from jax.experimental.pallas import tpu as pltpu
from jax.sharding import PartitionSpec as P

MESH = pl.DeviceIdType.MESH
BF16, F32, I32 = jnp.bfloat16, jnp.float32, jnp.int32

PANELS = 8
LANES = 128
CHUNK = 16

CROSS = 8
CUT = 13
CUT_REST = 16

def kernel(
    ab_sizes, cd_sizes, pairs_ref, amps_ref, ints_ref, out_ref,
    amps, ints, prod, from_core, x_one, x_two, from_y, cd_lab,
    g_send, g_recv, r_send, r_recv, local_sem,
):
    panel_rows, depth = amps_ref.shape
    ab_rows = ints_ref.shape[0]
    rounds = panel_rows // CHUNK
    lane_tiles = depth // LANES
    round_rows = PANELS * CHUNK

    ab, cd = lax.axis_index("ab"), lax.axis_index("cd")
    yl, z = ab // 4, lax.rem(ab, 4)
    x, yh, core = cd // 4, lax.rem(cd // 2, 2), lax.rem(cd, 2)
    z_up, z_down, z_far = lax.rem(z + 1, 4), lax.rem(z + 3, 4), lax.rem(z + 2, 4)
    mine, other = yl * 4, (1 - yl) * 4

    to_pair = {"ab": other + z, "cd": cd}
    to_up = {"ab": mine + z_up, "cd": cd}
    to_down = {"ab": mine + z_down, "cd": cd}
    to_core = {"ab": ab, "cd": x * 4 + yh * 2 + (1 - core)}
    to_y = {"ab": ab, "cd": x * 4 + (1 - yh) * 2 + core}
    to_right = {"ab": ab, "cd": lax.rem(x + 1, 4) * 4 + yh * 2 + core}
    to_left = {"ab": ab, "cd": lax.rem(x + 3, 4) * 4 + yh * 2 + core}

    def ints_copy(block):
        k, dc, dy = block // 4, 1 - (block // 2) % 2, block % 2
        dx = 2 + 3 * k - k * (k - 1) // 2
        part = lax.rem(x + dx, 4) * 4 + (yh + dy - 2 * yh * dy) * 2 + (core + dc - 2 * core * dc)
        start = pl.multiple_of(part * LANES, LANES)
        copy = pltpu.make_async_copy(
            ints_ref.at[pl.ds(start, LANES), :],
            ints.at[pl.ds(pl.multiple_of(block * LANES, LANES), LANES), :],
            local_sem.at[block],
        )
        return copy, start

    blocks = ab_rows // LANES

    @pl.loop(0, blocks)
    def _(block):
        ints_copy(block)[0].start()

    barrier = pltpu.get_barrier_semaphore()
    neighbours = (to_pair, to_up, to_down, to_core, to_y, to_right, to_left)
    for neighbour in neighbours:
        pl.semaphore_signal(barrier, inc=1, device_id=neighbour, device_id_type=MESH)
    pl.semaphore_wait(barrier, len(neighbours))

    def slot(q, owner, low, high):
        start = pl.multiple_of(q * round_rows + owner * CHUNK, CHUNK)
        return amps.at[pl.ds(start, CHUNK), pl.ds(low * LANES, (high - low) * LANES)]

    full, cross, rest = (0, lane_tiles), (0, CROSS), (CROSS, lane_tiles)
    low_cut, high_cut = (0, CUT), (CUT, lane_tiles)
    low_rest, high_rest = (CROSS, CUT_REST), (CUT_REST, lane_tiles)
    me, up, down, far = mine + z, mine + z_up, mine + z_down, mine + z_far
    o_me, o_up, o_down, o_far = other + z, other + z_up, other + z_down, other + z_far
    kinds = (
        (me, full, to_pair, o_me),
        (me, full, to_up, down),
        (me, full, to_down, up),
        (o_me, rest, to_up, o_down),
        (o_me, rest, to_down, o_up),
        (down, low_cut, to_up, far),
        (up, high_cut, to_down, far),
        (down, cross, to_pair, o_down),
        (up, cross, to_pair, o_up),
        (o_down, low_rest, to_up, o_far),
        (o_up, high_rest, to_down, o_far),
        (far, cross, to_pair, o_far),
    )

    def g_out(q, kind):
        owner, columns, target, _ = kinds[kind]
        ref = slot(q, owner, *columns)
        own = amps_ref.at[pl.ds(pl.multiple_of(q * CHUNK, CHUNK), CHUNK), :]
        return pltpu.make_async_remote_copy(
            src_ref=own if kind < 3 else ref, dst_ref=ref,
            send_sem=g_send.at[kind, q], recv_sem=g_recv.at[kind, q],
            device_id=target, device_id_type=MESH,
        )

    def g_in(q, kind):
        _, columns, target, owner = kinds[kind]
        ref = slot(q, owner, *columns)
        return pltpu.make_async_remote_copy(
            src_ref=ref, dst_ref=ref, send_sem=g_send.at[kind, q], recv_sem=g_recv.at[kind, q],
            device_id=target, device_id_type=MESH,
        )

    def first(q):
        for kind in (1, 2, 0):
            g_out(q, kind).start()

    def second(q):
        g_in(q, 1).wait_recv()
        g_out(q, 5).start()
        g_out(q, 7).start()
        g_in(q, 2).wait_recv()
        g_out(q, 6).start()
        g_out(q, 8).start()
        g_in(q, 0).wait_recv()
        g_out(q, 3).start()
        g_out(q, 4).start()

    def third(q):
        g_in(q, 5).wait_recv()
        g_out(q, 11).start()
        g_in(q, 3).wait_recv()
        g_out(q, 9).start()
        g_in(q, 4).wait_recv()
        g_out(q, 10).start()

    def arrived(q):
        for kind in (6, 7, 8, 9, 10, 11):
            g_in(q, kind).wait_recv()

    first(0)
    first(1)

    @pl.loop(0, rounds)
    def _(q):
        amps[pl.ds(pl.multiple_of(q * round_rows + me * CHUNK, CHUNK), CHUNK), :] = (
            amps_ref[pl.ds(pl.multiple_of(q * CHUNK, CHUNK), CHUNK), :]
        )

    def ends(sizes):
        out, total = [], jnp.int32(0)
        for k in range(sizes.shape[0]):
            total = total + sizes[k]
            out.append(total)
        return out

    def labels(where_at, limits):
        label = jnp.zeros(where_at.shape, I32)
        for limit in limits:
            label = label + (where_at >= limit).astype(I32)
        return label.astype(F32).astype(BF16)

    ab_ends, cd_ends = ends(ab_sizes), ends(cd_sizes)
    cd_lab[...] = labels(cd * depth + lax.broadcasted_iota(I32, cd_lab.shape, 1), cd_ends)

    def mask(block):
        copy, start = ints_copy(block)
        copy.wait()
        at = lax.broadcasted_iota(I32, (LANES, LANES), 0) + (ab * ab_rows + start)
        ab_lab = labels(at, ab_ends)

        def one(k, carry):
            columns = pl.ds(pl.multiple_of(k * LANES, LANES), LANES)
            rows = pl.ds(pl.multiple_of(block * LANES, LANES), LANES)
            here = jnp.broadcast_to(cd_lab[0:1, columns], (LANES, LANES))
            tile = ints[rows, columns]
            ints[rows, columns] = jnp.where(ab_lab == here, tile, jnp.zeros_like(tile))
            return carry

        lax.fori_loop(0, lane_tiles, one, 0, unroll=5)

    wide = 4 * LANES
    half = 2 * LANES

    def r_copy(g, kind, src, dst, target):
        return pltpu.make_async_remote_copy(
            src_ref=src, dst_ref=dst, send_sem=r_send.at[kind, g], recv_sem=r_recv.at[kind, g],
            device_id=target, device_id_type=MESH,
        )

    def core_copy(g, k):
        src = prod.at[g, pl.ds(pl.multiple_of(k * wide, wide), half), :]
        dst = from_core.at[g, pl.ds(pl.multiple_of(k * half, half), half), :]
        return r_copy(g, k, src, dst, to_core)

    def x_one_copy(g, way):
        src = prod.at[g, pl.ds(half + way * LANES, LANES), :]
        return r_copy(g, 4 + way, src, x_one.at[way, g], (to_right, to_left)[way])

    def x_two_copy(g, way):
        src = prod.at[g, pl.ds((1 + way) * wide + half, half), :]
        return r_copy(g, 6 + way, src, x_two.at[way, g], (to_right, to_left)[way])

    def y_copy(g):
        src = prod.at[g, pl.ds(3 * wide + half + LANES, LANES), :]
        return r_copy(g, 8, src, from_y.at[g], to_y)

    def kept(k):
        return pl.ds(k * wide + half, half)

    def product(g, part):
        columns = pl.ds(pl.multiple_of(part * 2 * wide, 2 * wide), 2 * wide)
        rows = pl.ds(pl.multiple_of(g * round_rows, round_rows), round_rows)
        prod[g, columns, :] = lax.dot_general(
            ints[columns, :], amps[rows, :], (((1,), (1,)), ((), ())), preferred_element_type=F32
        )
        core_copy(g, 2 * part).start()
        core_copy(g, 2 * part + 1).start()

    def x_first(g):
        core_copy(g, 0).wait_recv()
        prod[g, kept(0), :] += from_core[g, pl.ds(0, half), :]
        for way in range(2):
            x_one_copy(g, way).start()

    def x_second(g):
        for way in range(2):
            core_copy(g, 1 + way).wait_recv()
            prod[g, kept(1 + way), :] += from_core[g, pl.ds((1 + way) * half, half), :]
            x_one_copy(g, way).wait_recv()
            prod[g, pl.ds((1 + way) * wide + half + way * LANES, LANES), :] += x_one[way, g]
            x_two_copy(g, way).start()

    def y_step(g):
        core_copy(g, 3).wait_recv()
        total = prod[g, kept(3), :] + from_core[g, pl.ds(3 * half, half), :]
        x_two_copy(g, 0).wait_recv()
        x_two_copy(g, 1).wait_recv()
        prod[g, kept(3), :] = total + x_two[0, g] + x_two[1, g]
        y_copy(g).start()

    def place(g):
        y_copy(g).wait_recv()
        found = prod[g, pl.ds(3 * wide + half, LANES), :] + from_y[g]
        high = found.astype(BF16)
        left = found - high.astype(F32)
        mid = left.astype(BF16)
        low = (left - mid.astype(F32)).astype(BF16)
        target = jnp.broadcast_to(pairs_ref[pl.ds(g, 1), :], out_ref.shape)
        goes = lax.broadcasted_iota(I32, out_ref.shape, 0) == target
        goes = jnp.where(goes, 1.0, 0.0).astype(BF16)
        term = lax.dot_general(
            jnp.concatenate([goes, goes, goes], axis=1), jnp.concatenate([high, mid, low], axis=1),
            (((1,), (1,)), ((), ())), preferred_element_type=F32,
        )
        out_ref[...] += term

    def in_range(step, n):
        pl.when((n >= 0) & (n < rounds))(lambda: step(n))

    out_ref[...] = jnp.zeros_like(out_ref)

    @pl.loop(0, 2 * (rounds + 7))
    def _(h):
        q = h // 2

        @pl.when(h % 2 == 0)
        def _():
            in_range(second, q)
            in_range(first, q + 2)
            in_range(y_step, q - 6)
            in_range(x_first, q - 3)

        @pl.when(h % 2 == 1)
        def _():
            in_range(third, q - 1)
            in_range(arrived, q - 2)
            in_range(x_second, q - 4)
            in_range(place, q - 7)

        @pl.when(h < blocks // 4)
        def _():
            @pl.loop(0, 4)
            def _(block):
                mask(4 * h + block)

        in_range(lambda n: product(n, (h + 1) % 2), (h + 1) // 2 - 3)

    @pl.loop(0, rounds)
    def _(q):
        for kind in range(len(kinds)):
            g_out(q, kind).wait_send()
        for k in range(4):
            core_copy(q, k).wait_send()
        for way in range(2):
            x_one_copy(q, way).wait_send()
            x_two_copy(q, way).wait_send()
        y_copy(q).wait_send()


def shards(amplitudes, integrals, ab_sizes, cd_sizes, pair_index):
    panel_rows, depth = amplitudes.shape
    ab_rows = integrals.shape[0]
    all_pairs = pair_index.shape[0]
    rounds = panel_rows // CHUNK
    keeps = ab_rows // lax.axis_size("cd")
    pairs = pair_index.reshape(PANELS, rounds, CHUNK).transpose(1, 0, 2).reshape(rounds, PANELS * CHUNK)
    vmem, smem = pl.BlockSpec(memory_space=pltpu.VMEM), pl.BlockSpec(memory_space=pltpu.SMEM)
    return pl.pallas_call(
        kernel,
        out_shape=jax.ShapeDtypeStruct((all_pairs, keeps), F32),
        in_specs=[smem, smem, vmem, vmem, pl.BlockSpec(memory_space=pl.ANY)],
        out_specs=vmem,
        scratch_shapes=[
            pltpu.VMEM((all_pairs, depth), BF16),
            pltpu.VMEM((ab_rows, depth), BF16),
            pltpu.VMEM((rounds, ab_rows, PANELS * CHUNK), F32),
            pltpu.VMEM((rounds, ab_rows // 2, PANELS * CHUNK), F32),
            pltpu.VMEM((2, rounds, keeps, PANELS * CHUNK), F32),
            pltpu.VMEM((2, rounds, 2 * keeps, PANELS * CHUNK), F32),
            pltpu.VMEM((rounds, keeps, PANELS * CHUNK), F32),
            pltpu.VMEM((16, depth), BF16),
            pltpu.SemaphoreType.DMA((12, rounds)),
            pltpu.SemaphoreType.DMA((12, rounds)),
            pltpu.SemaphoreType.DMA((9, rounds)),
            pltpu.SemaphoreType.DMA((9, rounds)),
            pltpu.SemaphoreType.DMA((ab_rows // LANES,)),
        ],
        name="ladder",
        compiler_params=pltpu.CompilerParams(
            collective_id=0, has_side_effects=True, vmem_limit_bytes=56 << 20
        ),
    )(ab_sizes, cd_sizes, pairs, amplitudes, integrals)


def solution(mesh):
    return jax.shard_map(
        shards,
        mesh=mesh,
        in_specs=(P("ab", "cd"), P("ab", "cd"), P(), P(), P()),
        out_specs=P(None, ("ab", "cd")),
        check_vma=False,
    )
```

```python
import functools

import jax
import jax.numpy as jnp
from jax import lax
from jax.experimental import pallas as pl
from jax.experimental.pallas import tpu as pltpu
from jax.sharding import PartitionSpec as P

MESH = pl.DeviceIdType.MESH
BF16, F32, I32 = jnp.bfloat16, jnp.float32, jnp.int32

PANELS = 8
LANES = 128
CHUNK = 16

CROSS = 10
CUT = 13
CUT_REST = 17

STAGES = (
    (("third", 1), ("second", 0), ("first", -2), ("y", 5), ("x one", 2)),
    (("arrived", 1), ("x two", 3), ("place", 6)),
)
MULTIPLY = 3
LATE = 2

def encode(values):
    largest = jnp.maximum(jnp.max(jnp.abs(values), axis=0, keepdims=True), 1e-30)
    size = jnp.ceil(jnp.log2(largest) * 16.0) + 1.0
    codes = jnp.round(values * (jnp.exp2(size * -0.0625) * 32000.0)).astype(I32)
    sizes = jnp.broadcast_to(size, (CHUNK, values.shape[1])).astype(I32)
    return jnp.concatenate([codes, sizes], axis=0).astype(jnp.int16)


def decode(codes):
    codes = codes.astype(I32).astype(F32)
    rows = codes.shape[0] - CHUNK
    return codes[:rows] * (jnp.exp2(codes[rows : rows + 1] * 0.0625) * (1.0 / 32000.0))


def kernel(
    ab_sizes, cd_sizes, pairs_ref, amps_ref, ints_ref, out_ref,
    amps, ints, prod, from_core, x_one, x_two, from_y, cd_lab,
    x_one_out, x_two_out, y_out,
    g_send, g_recv, r_send, r_recv, local_sem,
):
    panel_rows, depth = amps_ref.shape
    ab_rows = ints_ref.shape[0]
    rounds = panel_rows // CHUNK
    lane_tiles = depth // LANES
    round_rows = PANELS * CHUNK

    ab, cd = lax.axis_index("ab"), lax.axis_index("cd")
    yl, z = ab // 4, lax.rem(ab, 4)
    x, yh, core = cd // 4, lax.rem(cd // 2, 2), lax.rem(cd, 2)
    z_up, z_down, z_far = lax.rem(z + 1, 4), lax.rem(z + 3, 4), lax.rem(z + 2, 4)
    mine, other = yl * 4, (1 - yl) * 4

    to_pair = {"ab": other + z, "cd": cd}
    to_up = {"ab": mine + z_up, "cd": cd}
    to_down = {"ab": mine + z_down, "cd": cd}
    to_core = {"ab": ab, "cd": x * 4 + yh * 2 + (1 - core)}
    to_y = {"ab": ab, "cd": x * 4 + (1 - yh) * 2 + core}
    to_right = {"ab": ab, "cd": lax.rem(x + 1, 4) * 4 + yh * 2 + core}
    to_left = {"ab": ab, "cd": lax.rem(x + 3, 4) * 4 + yh * 2 + core}

    def ints_copy(block):
        k, dc, dy = block // 4, 1 - (block // 2) % 2, block % 2
        dx = 2 + 3 * k - k * (k - 1) // 2
        part = lax.rem(x + dx, 4) * 4 + (yh + dy - 2 * yh * dy) * 2 + (core + dc - 2 * core * dc)
        start = pl.multiple_of(part * LANES, LANES)
        copy = pltpu.make_async_copy(
            ints_ref.at[pl.ds(start, LANES), :],
            ints.at[pl.ds(pl.multiple_of(block * LANES, LANES), LANES), :],
            local_sem.at[block],
        )
        return copy, start

    blocks = ab_rows // LANES

    @pl.loop(0, blocks)
    def _(block):
        ints_copy(block)[0].start()

    barrier = pltpu.get_barrier_semaphore()
    neighbours = (to_pair, to_up, to_down, to_core, to_y, to_right, to_left)
    for neighbour in neighbours:
        pl.semaphore_signal(barrier, inc=1, device_id=neighbour, device_id_type=MESH)
    pl.semaphore_wait(barrier, len(neighbours))

    def slot(q, owner, low, high):
        start = pl.multiple_of(q * round_rows + owner * CHUNK, CHUNK)
        return amps.at[pl.ds(start, CHUNK), pl.ds(low * LANES, (high - low) * LANES)]

    full, cross, rest = (0, lane_tiles), (0, CROSS), (CROSS, lane_tiles)
    low_cut, high_cut = (0, CUT), (CUT, lane_tiles)
    low_rest, high_rest = (CROSS, CUT_REST), (CUT_REST, lane_tiles)
    me, up, down, far = mine + z, mine + z_up, mine + z_down, mine + z_far
    o_me, o_up, o_down, o_far = other + z, other + z_up, other + z_down, other + z_far
    kinds = (
        (me, full, to_pair, o_me),
        (me, full, to_up, down),
        (me, full, to_down, up),
        (o_me, rest, to_up, o_down),
        (o_me, rest, to_down, o_up),
        (down, low_cut, to_up, far),
        (up, high_cut, to_down, far),
        (down, cross, to_pair, o_down),
        (up, cross, to_pair, o_up),
        (o_down, low_rest, to_up, o_far),
        (o_up, high_rest, to_down, o_far),
        (far, cross, to_pair, o_far),
    )

    def g_out(q, kind):
        owner, columns, target, _ = kinds[kind]
        ref = slot(q, owner, *columns)
        own = amps_ref.at[pl.ds(pl.multiple_of(q * CHUNK, CHUNK), CHUNK), :]
        return pltpu.make_async_remote_copy(
            src_ref=own if kind < 3 else ref, dst_ref=ref,
            send_sem=g_send.at[kind, q], recv_sem=g_recv.at[kind, q],
            device_id=target, device_id_type=MESH,
        )

    def g_in(q, kind):
        _, columns, target, owner = kinds[kind]
        ref = slot(q, owner, *columns)
        return pltpu.make_async_remote_copy(
            src_ref=ref, dst_ref=ref, send_sem=g_send.at[kind, q], recv_sem=g_recv.at[kind, q],
            device_id=target, device_id_type=MESH,
        )

    def first(q):
        for kind in (1, 2, 0):
            g_out(q, kind).start()

    def second(q):
        g_in(q, 1).wait_recv()
        g_out(q, 5).start()
        g_out(q, 7).start()
        g_in(q, 2).wait_recv()
        g_out(q, 6).start()
        g_out(q, 8).start()
        g_in(q, 0).wait_recv()
        g_out(q, 3).start()
        g_out(q, 4).start()

    def third(q):
        g_in(q, 5).wait_recv()
        g_out(q, 11).start()
        g_in(q, 3).wait_recv()
        g_out(q, 9).start()
        g_in(q, 4).wait_recv()
        g_out(q, 10).start()

    def arrived(q):
        for kind in (6, 7, 8, 9, 10, 11):
            g_in(q, kind).wait_recv()

    first(0)
    first(1)

    @pl.loop(0, rounds)
    def _(q):
        amps[pl.ds(pl.multiple_of(q * round_rows + me * CHUNK, CHUNK), CHUNK), :] = (
            amps_ref[pl.ds(pl.multiple_of(q * CHUNK, CHUNK), CHUNK), :]
        )

    def ends(sizes):
        out, total = [], jnp.int32(0)
        for k in range(sizes.shape[0]):
            total = total + sizes[k]
            out.append(total)
        return out

    def labels(where_at, limits):
        label = jnp.zeros(where_at.shape, I32)
        for limit in limits:
            label = label + (where_at >= limit).astype(I32)
        return label.astype(F32).astype(BF16)

    ab_ends, cd_ends = ends(ab_sizes), ends(cd_sizes)
    cd_lab[...] = labels(cd * depth + lax.broadcasted_iota(I32, cd_lab.shape, 1), cd_ends)

    def mask(block):
        copy, start = ints_copy(block)
        copy.wait()
        at = lax.broadcasted_iota(I32, (LANES, LANES), 0) + (ab * ab_rows + start)
        ab_lab = labels(at, ab_ends)

        def one(k, carry):
            columns = pl.ds(pl.multiple_of(k * LANES, LANES), LANES)
            rows = pl.ds(pl.multiple_of(block * LANES, LANES), LANES)
            here = jnp.broadcast_to(cd_lab[0:1, columns], (LANES, LANES))
            tile = ints[rows, columns]
            ints[rows, columns] = jnp.where(ab_lab == here, tile, jnp.zeros_like(tile))
            return carry

        lax.fori_loop(0, lane_tiles, one, 0, unroll=5)

    wide = 4 * LANES
    half = 2 * LANES

    def r_copy(g, kind, src, dst, target):
        return pltpu.make_async_remote_copy(
            src_ref=src, dst_ref=dst, send_sem=r_send.at[kind, g], recv_sem=r_recv.at[kind, g],
            device_id=target, device_id_type=MESH,
        )

    def core_copy(g, k):
        src = prod.at[g, pl.ds(pl.multiple_of(k * wide, wide), half), :]
        dst = from_core.at[g, pl.ds(pl.multiple_of(k * half, half), half), :]
        return r_copy(g, k, src, dst, to_core)

    def x_one_copy(g, way):
        return r_copy(g, 4 + way, x_one_out.at[way, g], x_one.at[way, g], (to_right, to_left)[way])

    def x_two_copy(g, way):
        return r_copy(g, 6 + way, x_two_out.at[way, g], x_two.at[way, g], (to_right, to_left)[way])

    def y_copy(g):
        return r_copy(g, 8, y_out.at[g], from_y.at[g], to_y)

    def kept(k):
        return pl.ds(k * wide + half, half)

    def product(g, part, count):
        columns = pl.ds(pl.multiple_of(part * 2 * wide, 2 * wide), 2 * wide)
        rows = pl.ds(pl.multiple_of(g * round_rows, round_rows), count * round_rows)
        found = lax.dot_general(
            ints[columns, :], amps[rows, :], (((1,), (1,)), ((), ())), preferred_element_type=F32
        )
        for one in range(count):
            prod[g + one, columns, :] = found[:, one * round_rows : (one + 1) * round_rows]
        for k in range(2):
            for one in range(count):
                core_copy(g + one, 2 * part + k).start()

    def x_first(g):
        core_copy(g, 0).wait_recv()
        for way in range(2):
            at = half + way * LANES
            part = prod[g, pl.ds(at, LANES), :] + from_core[g, pl.ds(way * LANES, LANES), :]
            x_one_out[way, g] = encode(part)
            x_one_copy(g, way).start()

    def x_second(g):
        for way in range(2):
            core_copy(g, 1 + way).wait_recv()
            part = prod[g, kept(1 + way), :] + from_core[g, pl.ds((1 + way) * half, half), :]
            x_one_copy(g, way).wait_recv()
            more = decode(x_one[way, g])
            low, high = part[:LANES], part[LANES:]
            low, high = (low, high + more) if way else (low + more, high)
            x_two_out[way, g] = encode(jnp.concatenate([low, high], axis=0))
            x_two_copy(g, way).start()

    def y_step(g):
        core_copy(g, 3).wait_recv()
        total = prod[g, kept(3), :] + from_core[g, pl.ds(3 * half, half), :]
        x_two_copy(g, 0).wait_recv()
        x_two_copy(g, 1).wait_recv()
        total = total + decode(x_two[0, g]) + decode(x_two[1, g])
        y_out[g] = encode(total[LANES:])
        y_copy(g).start()
        prod[g, pl.ds(3 * wide + half, LANES), :] = total[:LANES]

    def place(g):
        y_copy(g).wait_recv()
        found = prod[g, pl.ds(3 * wide + half, LANES), :] + decode(from_y[g])
        high = found.astype(BF16)
        left = found - high.astype(F32)
        mid = left.astype(BF16)
        low = (left - mid.astype(F32)).astype(BF16)
        shape = (out_ref.shape[0], round_rows)
        target = jnp.broadcast_to(pairs_ref[pl.ds(g, 1), :], shape)
        goes = lax.broadcasted_iota(I32, shape, 0) == target
        goes = jnp.where(goes, 1.0, 0.0).astype(BF16)
        term = lax.dot_general(
            jnp.concatenate([goes, goes, goes], axis=1), jnp.concatenate([high, mid, low], axis=1),
            (((1,), (1,)), ((), ())), preferred_element_type=F32,
        )
        out_ref[...] += term

    def in_range(step, n):
        pl.when((n >= 0) & (n < rounds))(lambda: step(n))

    late = rounds - LATE

    def together(step, n):
        @pl.when((n >= 0) & (n < rounds) & ((n >= late) | (n % 2 == 1)))
        def _():
            pl.loop(n - (n < late).astype(I32), n + 1)(step)

    does = {
        "first": functools.partial(in_range, first),
        "second": functools.partial(in_range, second),
        "third": functools.partial(in_range, third),
        "arrived": functools.partial(in_range, arrived),
        "x one": functools.partial(together, x_first),
        "x two": functools.partial(together, x_second),
        "y": functools.partial(together, y_step),
        "place": functools.partial(together, place),
    }
    out_ref[...] = jnp.zeros_like(out_ref)

    @pl.loop(0, 2 * (rounds + 7))
    def _(h):
        q = h // 2

        for parity in range(2):

            @pl.when(h % 2 == parity)
            def _():
                for name, lag in STAGES[parity]:
                    does[name](q - lag)

        @pl.when(h < blocks // 4)
        def _():
            @pl.loop(0, 4)
            def _(block):
                mask(4 * h + block)

        ready, part = (h + 8 - MULTIPLY) // 2 - 4, (h + 8 - MULTIPLY) % 2

        @pl.when((ready >= late) & (ready < rounds))
        def _():
            product(ready, part, 1)

        @pl.when((ready >= 0) & (ready < late) & (ready % 2 == 1))
        def _():
            product(ready - 1, part, 2)

    @pl.loop(0, rounds)
    def _(q):
        for kind in range(len(kinds)):
            g_out(q, kind).wait_send()
        for k in range(4):
            core_copy(q, k).wait_send()
        for way in range(2):
            x_one_copy(q, way).wait_send()
            x_two_copy(q, way).wait_send()
        y_copy(q).wait_send()


def shards(amplitudes, integrals, ab_sizes, cd_sizes, pair_index):
    panel_rows, depth = amplitudes.shape
    ab_rows = integrals.shape[0]
    all_pairs = pair_index.shape[0]
    rounds = panel_rows // CHUNK
    keeps = ab_rows // lax.axis_size("cd")
    pairs = pair_index.reshape(PANELS, rounds, CHUNK).transpose(1, 0, 2).reshape(rounds, PANELS * CHUNK)
    sums = (
        pltpu.VMEM((2, rounds, keeps + CHUNK, PANELS * CHUNK), jnp.int16),
        pltpu.VMEM((2, rounds, 2 * keeps + CHUNK, PANELS * CHUNK), jnp.int16),
        pltpu.VMEM((rounds, keeps + CHUNK, PANELS * CHUNK), jnp.int16),
    )
    vmem, smem = pl.BlockSpec(memory_space=pltpu.VMEM), pl.BlockSpec(memory_space=pltpu.SMEM)
    return pl.pallas_call(
        kernel,
        out_shape=jax.ShapeDtypeStruct((all_pairs, keeps), F32),
        in_specs=[smem, smem, vmem, vmem, pl.BlockSpec(memory_space=pl.ANY)],
        out_specs=vmem,
        scratch_shapes=[
            pltpu.VMEM((all_pairs, depth), BF16),
            pltpu.VMEM((ab_rows, depth), BF16),
            pltpu.VMEM((rounds, ab_rows, PANELS * CHUNK), F32),
            pltpu.VMEM((rounds, ab_rows // 2, PANELS * CHUNK), F32),
            *sums,
            pltpu.VMEM((16, depth), BF16),
            *sums,
            pltpu.SemaphoreType.DMA((12, rounds)),
            pltpu.SemaphoreType.DMA((12, rounds)),
            pltpu.SemaphoreType.DMA((9, rounds)),
            pltpu.SemaphoreType.DMA((9, rounds)),
            pltpu.SemaphoreType.DMA((ab_rows // LANES,)),
        ],
        name="ladder",
        compiler_params=pltpu.CompilerParams(
            collective_id=0, has_side_effects=True, vmem_limit_bytes=56 << 20
        ),
    )(ab_sizes, cd_sizes, pairs, amplitudes, integrals)


def solution(mesh):
    return jax.shard_map(
        shards,
        mesh=mesh,
        in_specs=(P("ab", "cd"), P("ab", "cd"), P(), P(), P()),
        out_specs=P(None, ("ab", "cd")),
        check_vma=False,
    )
```

```python
import functools

import jax
import jax.numpy as jnp
from jax import lax
from jax.experimental import pallas as pl
from jax.experimental.pallas import tpu as pltpu
from jax.sharding import PartitionSpec as P

MESH = pl.DeviceIdType.MESH
BF16, F32, I32 = jnp.bfloat16, jnp.float32, jnp.int32

PANELS = 8
LANES = 128
CHUNK = 16

CROSS = 10
CUT = 13
CUT_REST = 17

STAGES = (
    (("third", 1), ("second", 0), ("first", -2), ("y", 5), ("x one", 2)),
    (("arrived", 1), ("x two", 3), ("place", 6)),
)
MULTIPLY = 3
LATE = 2

def encode(values):
    largest = jnp.maximum(jnp.max(jnp.abs(values), axis=0, keepdims=True), 1e-30)
    size = jnp.ceil(jnp.log2(largest) * 16.0) + 1.0
    codes = jnp.round(values * (jnp.exp2(size * -0.0625) * 32000.0)).astype(I32)
    sizes = jnp.broadcast_to(size, (CHUNK, values.shape[1])).astype(I32)
    return jnp.concatenate([codes, sizes], axis=0).astype(jnp.int16)


def decode(codes):
    codes = codes.astype(I32).astype(F32)
    rows = codes.shape[0] - CHUNK
    return codes[:rows] * (jnp.exp2(codes[rows : rows + 1] * 0.0625) * (1.0 / 32000.0))


def kernel(
    ab_sizes, cd_sizes, pairs_ref, amps_ref, ints_ref, out_ref,
    amps, ints, prod, from_core, x_one, x_two, from_y, cd_lab,
    x_one_out, x_two_out, y_out, targets,
    g_send, g_recv, r_send, r_recv, local_sem,
):
    panel_rows, depth = amps_ref.shape
    ab_rows = ints_ref.shape[0]
    rounds = panel_rows // CHUNK
    lane_tiles = depth // LANES
    round_rows = PANELS * CHUNK

    ab, cd = lax.axis_index("ab"), lax.axis_index("cd")
    yl, z = ab // 4, lax.rem(ab, 4)
    x, yh, core = cd // 4, lax.rem(cd // 2, 2), lax.rem(cd, 2)
    z_up, z_down, z_far = lax.rem(z + 1, 4), lax.rem(z + 3, 4), lax.rem(z + 2, 4)
    mine, other = yl * 4, (1 - yl) * 4

    to_pair = {"ab": other + z, "cd": cd}
    to_up = {"ab": mine + z_up, "cd": cd}
    to_down = {"ab": mine + z_down, "cd": cd}
    to_core = {"ab": ab, "cd": x * 4 + yh * 2 + (1 - core)}
    to_y = {"ab": ab, "cd": x * 4 + (1 - yh) * 2 + core}
    to_right = {"ab": ab, "cd": lax.rem(x + 1, 4) * 4 + yh * 2 + core}
    to_left = {"ab": ab, "cd": lax.rem(x + 3, 4) * 4 + yh * 2 + core}

    def ints_copy(block):
        k, dc, dy = block // 4, 1 - (block // 2) % 2, block % 2
        dx = 2 + 3 * k - k * (k - 1) // 2
        part = lax.rem(x + dx, 4) * 4 + (yh + dy - 2 * yh * dy) * 2 + (core + dc - 2 * core * dc)
        start = pl.multiple_of(part * LANES, LANES)
        copy = pltpu.make_async_copy(
            ints_ref.at[pl.ds(start, LANES), :],
            ints.at[pl.ds(pl.multiple_of(block * LANES, LANES), LANES), :],
            local_sem.at[block],
        )
        return copy, start

    blocks = ab_rows // LANES

    @pl.loop(0, blocks)
    def _(block):
        ints_copy(block)[0].start()

    barrier = pltpu.get_barrier_semaphore()
    neighbours = (to_pair, to_up, to_down, to_core, to_y, to_right, to_left)
    for neighbour in neighbours:
        pl.semaphore_signal(barrier, inc=1, device_id=neighbour, device_id_type=MESH)
    pl.semaphore_wait(barrier, len(neighbours))

    def slot(q, owner, low, high):
        start = pl.multiple_of(q * round_rows + owner * CHUNK, CHUNK)
        return amps.at[pl.ds(start, CHUNK), pl.ds(low * LANES, (high - low) * LANES)]

    full, cross, rest = (0, lane_tiles), (0, CROSS), (CROSS, lane_tiles)
    low_cut, high_cut = (0, CUT), (CUT, lane_tiles)
    low_rest, high_rest = (CROSS, CUT_REST), (CUT_REST, lane_tiles)
    me, up, down, far = mine + z, mine + z_up, mine + z_down, mine + z_far
    o_me, o_up, o_down, o_far = other + z, other + z_up, other + z_down, other + z_far
    kinds = (
        (me, full, to_pair, o_me),
        (me, full, to_up, down),
        (me, full, to_down, up),
        (o_me, rest, to_up, o_down),
        (o_me, rest, to_down, o_up),
        (down, low_cut, to_up, far),
        (up, high_cut, to_down, far),
        (down, cross, to_pair, o_down),
        (up, cross, to_pair, o_up),
        (o_down, low_rest, to_up, o_far),
        (o_up, high_rest, to_down, o_far),
        (far, cross, to_pair, o_far),
    )

    def g_out(q, kind):
        owner, columns, target, _ = kinds[kind]
        ref = slot(q, owner, *columns)
        own = amps_ref.at[pl.ds(pl.multiple_of(q * CHUNK, CHUNK), CHUNK), :]
        return pltpu.make_async_remote_copy(
            src_ref=own if kind < 3 else ref, dst_ref=ref,
            send_sem=g_send.at[kind, q], recv_sem=g_recv.at[kind, q],
            device_id=target, device_id_type=MESH,
        )

    def g_in(q, kind):
        _, columns, target, owner = kinds[kind]
        ref = slot(q, owner, *columns)
        return pltpu.make_async_remote_copy(
            src_ref=ref, dst_ref=ref, send_sem=g_send.at[kind, q], recv_sem=g_recv.at[kind, q],
            device_id=target, device_id_type=MESH,
        )

    def first(q):
        for kind in (1, 2, 0):
            g_out(q, kind).start()

    def second(q):
        g_in(q, 1).wait_recv()
        g_out(q, 5).start()
        g_out(q, 7).start()
        g_in(q, 2).wait_recv()
        g_out(q, 6).start()
        g_out(q, 8).start()
        g_in(q, 0).wait_recv()
        g_out(q, 3).start()
        g_out(q, 4).start()

    def third(q):
        g_in(q, 5).wait_recv()
        g_out(q, 11).start()
        g_in(q, 3).wait_recv()
        g_out(q, 9).start()
        g_in(q, 4).wait_recv()
        g_out(q, 10).start()

    def arrived(q):
        own_copy(q).wait()
        for kind in (6, 7, 8, 9, 10, 11):
            g_in(q, kind).wait_recv()

    def own_copy(q):
        return pltpu.make_async_copy(
            amps_ref.at[pl.ds(pl.multiple_of(q * CHUNK, CHUNK), CHUNK), :],
            slot(q, me, *full),
            local_sem.at[blocks + q],
        )

    first(0)
    first(1)

    @pl.loop(0, rounds)
    def _(q):
        own_copy(q).start()

    def ends(sizes):
        out, total = [], jnp.int32(0)
        for k in range(sizes.shape[0]):
            total = total + sizes[k]
            out.append(total)
        return out

    def labels(where_at, limits):
        label = jnp.zeros(where_at.shape, I32)
        for limit in limits:
            label = label + (where_at >= limit).astype(I32)
        return label.astype(F32).astype(BF16)

    ab_ends, cd_ends = ends(ab_sizes), ends(cd_sizes)
    cd_lab[...] = labels(cd * depth + lax.broadcasted_iota(I32, cd_lab.shape, 1), cd_ends)

    def mask(block):
        copy, start = ints_copy(block)
        copy.wait()
        at = lax.broadcasted_iota(I32, (LANES, LANES), 0) + (ab * ab_rows + start)
        ab_lab = labels(at, ab_ends)

        def one(k, carry):
            columns = pl.ds(pl.multiple_of(k * LANES, LANES), LANES)
            rows = pl.ds(pl.multiple_of(block * LANES, LANES), LANES)
            here = jnp.broadcast_to(cd_lab[0:1, columns], (LANES, LANES))
            tile = ints[rows, columns]
            ints[rows, columns] = jnp.where(ab_lab == here, tile, jnp.zeros_like(tile))
            return carry

        lax.fori_loop(0, lane_tiles, one, 0, unroll=5)

    wide = 4 * LANES
    half = 2 * LANES

    def r_copy(g, kind, src, dst, target):
        return pltpu.make_async_remote_copy(
            src_ref=src, dst_ref=dst, send_sem=r_send.at[kind, g], recv_sem=r_recv.at[kind, g],
            device_id=target, device_id_type=MESH,
        )

    def core_copy(g, k):
        src = prod.at[g, pl.ds(pl.multiple_of(k * wide, wide), half), :]
        dst = from_core.at[g, pl.ds(pl.multiple_of(k * half, half), half), :]
        return r_copy(g, k, src, dst, to_core)

    def x_one_copy(g, way):
        return r_copy(g, 4 + way, x_one_out.at[way, g], x_one.at[way, g], (to_right, to_left)[way])

    def x_two_copy(g, way):
        return r_copy(g, 6 + way, x_two_out.at[way, g], x_two.at[way, g], (to_right, to_left)[way])

    def y_copy(g):
        return r_copy(g, 8, y_out.at[g], from_y.at[g], to_y)

    def kept(k):
        return pl.ds(k * wide + half, half)

    def product(g, part, count):
        columns = pl.ds(pl.multiple_of(part * 2 * wide, 2 * wide), 2 * wide)
        rows = pl.ds(pl.multiple_of(g * round_rows, round_rows), count * round_rows)
        found = lax.dot_general(
            ints[columns, :], amps[rows, :], (((1,), (1,)), ((), ())), preferred_element_type=F32
        )
        for one in range(count):
            prod[g + one, columns, :] = found[:, one * round_rows : (one + 1) * round_rows]
        for k in range(2):
            for one in range(count):
                core_copy(g + one, 2 * part + k).start()

    def x_first(g):
        core_copy(g, 0).wait_recv()
        for way in range(2):
            at = half + way * LANES
            part = prod[g, pl.ds(at, LANES), :] + from_core[g, pl.ds(way * LANES, LANES), :]
            x_one_out[way, g] = encode(part)
            x_one_copy(g, way).start()

    def x_second(g):
        for way in range(2):
            core_copy(g, 1 + way).wait_recv()
            part = prod[g, kept(1 + way), :] + from_core[g, pl.ds((1 + way) * half, half), :]
            x_one_copy(g, way).wait_recv()
            more = decode(x_one[way, g])
            low, high = part[:LANES], part[LANES:]
            low, high = (low, high + more) if way else (low + more, high)
            x_two_out[way, g] = encode(jnp.concatenate([low, high], axis=0))
            x_two_copy(g, way).start()

    def y_step(g):
        core_copy(g, 3).wait_recv()
        total = prod[g, kept(3), :] + from_core[g, pl.ds(3 * half, half), :]
        x_two_copy(g, 0).wait_recv()
        x_two_copy(g, 1).wait_recv()
        total = total + decode(x_two[0, g]) + decode(x_two[1, g])
        y_out[g] = encode(total[LANES:])
        y_copy(g).start()
        prod[g, pl.ds(3 * wide + half, LANES), :] = total[:LANES]

    def place(g):
        y_copy(g).wait_recv()
        found = prod[g, pl.ds(3 * wide + half, LANES), :] + decode(from_y[g])
        high = found.astype(BF16)
        left = found - high.astype(F32)
        mid = left.astype(BF16)
        low = (left - mid.astype(F32)).astype(BF16)
        shape = (out_ref.shape[0], round_rows)
        target = jnp.broadcast_to(targets[pl.ds(g, 1), :], shape)
        goes = lax.broadcasted_iota(I32, shape, 0) == target
        goes = jnp.where(goes, 1.0, 0.0).astype(BF16)
        term = lax.dot_general(
            jnp.concatenate([goes, goes, goes], axis=1), jnp.concatenate([high, mid, low], axis=1),
            (((1,), (1,)), ((), ())), preferred_element_type=F32,
        )
        out_ref[...] += term
        for kind in range(len(kinds)):
            g_out(g, kind).wait_send()
        for k in range(4):
            core_copy(g, k).wait_send()
        for way in range(2):
            x_one_copy(g, way).wait_send()
            x_two_copy(g, way).wait_send()
        y_copy(g).wait_send()

    pairs = pairs_ref[...]
    chunk = lax.broadcasted_iota(I32, pairs.shape, 1) // CHUNK
    panel = lax.broadcasted_iota(I32, pairs.shape, 0)
    turned = [pairs if m == 0 else pltpu.roll(pairs, m * CHUNK, 1) for m in range(rounds)]
    for g in range(rounds):
        chosen = jnp.zeros_like(pairs)
        for p in range(PANELS):
            chosen = jnp.where((panel == p) & (chunk == p), turned[(p - g) % rounds], chosen)
        targets[g : g + 1, :] = jnp.sum(chosen, axis=0, keepdims=True)

    def in_range(step, n):
        pl.when((n >= 0) & (n < rounds))(lambda: step(n))

    late = rounds - LATE

    def together(step, n):
        @pl.when((n >= 0) & (n < rounds) & ((n >= late) | (n % 2 == 1)))
        def _():
            pl.loop(n - (n < late).astype(I32), n + 1)(step)

    does = {
        "first": functools.partial(in_range, first),
        "second": functools.partial(in_range, second),
        "third": functools.partial(in_range, third),
        "arrived": functools.partial(in_range, arrived),
        "x one": functools.partial(together, x_first),
        "x two": functools.partial(together, x_second),
        "y": functools.partial(together, y_step),
        "place": functools.partial(together, place),
    }
    out_ref[...] = jnp.zeros_like(out_ref)

    @pl.loop(0, 2 * (rounds + 7))
    def _(h):
        q = h // 2

        for parity in range(2):

            @pl.when(h % 2 == parity)
            def _():
                for name, lag in STAGES[parity]:
                    does[name](q - lag)

        @pl.when(h < blocks // 4)
        def _():
            @pl.loop(0, 4)
            def _(block):
                mask(4 * h + block)

        ready, part = (h + 8 - MULTIPLY) // 2 - 4, (h + 8 - MULTIPLY) % 2

        @pl.when((ready >= late) & (ready < rounds))
        def _():
            product(ready, part, 1)

        @pl.when((ready >= 0) & (ready < late) & (ready % 2 == 1))
        def _():
            product(ready - 1, part, 2)


def shards(amplitudes, integrals, ab_sizes, cd_sizes, pair_index):
    panel_rows, depth = amplitudes.shape
    ab_rows = integrals.shape[0]
    all_pairs = pair_index.shape[0]
    rounds = panel_rows // CHUNK
    keeps = ab_rows // lax.axis_size("cd")
    pairs = pair_index.reshape(PANELS, panel_rows)
    sums = (
        pltpu.VMEM((2, rounds, keeps + CHUNK, PANELS * CHUNK), jnp.int16),
        pltpu.VMEM((2, rounds, 2 * keeps + CHUNK, PANELS * CHUNK), jnp.int16),
        pltpu.VMEM((rounds, keeps + CHUNK, PANELS * CHUNK), jnp.int16),
    )
    vmem, smem = pl.BlockSpec(memory_space=pltpu.VMEM), pl.BlockSpec(memory_space=pltpu.SMEM)
    hbm = pl.BlockSpec(memory_space=pl.ANY)
    return pl.pallas_call(
        kernel,
        out_shape=jax.ShapeDtypeStruct((all_pairs, keeps), F32),
        in_specs=[smem, smem, vmem, hbm, hbm],
        out_specs=vmem,
        scratch_shapes=[
            pltpu.VMEM((all_pairs, depth), BF16),
            pltpu.VMEM((ab_rows, depth), BF16),
            pltpu.VMEM((rounds, ab_rows, PANELS * CHUNK), F32),
            pltpu.VMEM((rounds, ab_rows // 2, PANELS * CHUNK), F32),
            *sums,
            pltpu.VMEM((16, depth), BF16),
            *sums,
            pltpu.VMEM((rounds, PANELS * CHUNK), I32),
            pltpu.SemaphoreType.DMA((12, rounds)),
            pltpu.SemaphoreType.DMA((12, rounds)),
            pltpu.SemaphoreType.DMA((9, rounds)),
            pltpu.SemaphoreType.DMA((9, rounds)),
            pltpu.SemaphoreType.DMA((ab_rows // LANES + rounds,)),
        ],
        name="ladder",
        compiler_params=pltpu.CompilerParams(
            collective_id=0, has_side_effects=True, vmem_limit_bytes=56 << 20
        ),
    )(ab_sizes, cd_sizes, pairs, amplitudes, integrals)


def solution(mesh):
    return jax.shard_map(
        shards,
        mesh=mesh,
        in_specs=(P("ab", "cd"), P("ab", "cd"), P(), P(), P()),
        out_specs=P(None, ("ab", "cd")),
        check_vma=False,
    )
```

```python
import functools

import jax
import jax.numpy as jnp
from jax import lax
from jax.experimental import pallas as pl
from jax.experimental.pallas import tpu as pltpu
from jax.sharding import PartitionSpec as P

MESH = pl.DeviceIdType.MESH
BF16, F32, I32 = jnp.bfloat16, jnp.float32, jnp.int32

PANELS = 8
LANES = 128
CHUNK = 16

CROSS = 10
CUT = 13
CUT_REST = 17

STAGES = (
    (("third", 1), ("second", 0), ("first", -2), ("y", 6), ("x one", 2)),
    (("arrived", 1), ("x two", 3), ("place", 8)),
)
MULTIPLY = 3
DRAIN = 8
LATE = 2

def encode(values):
    largest = jnp.maximum(jnp.max(jnp.abs(values), axis=0, keepdims=True), 1e-30)
    size = jnp.ceil(jnp.log2(largest) * 16.0) + 1.0
    codes = jnp.round(values * (jnp.exp2(size * -0.0625) * 32000.0)).astype(I32)
    sizes = jnp.broadcast_to(size, (CHUNK, values.shape[1])).astype(I32)
    return jnp.concatenate([codes, sizes], axis=0).astype(jnp.int16)


def decode(codes):
    codes = codes.astype(I32).astype(F32)
    rows = codes.shape[0] - CHUNK
    return codes[:rows] * (jnp.exp2(codes[rows : rows + 1] * 0.0625) * (1.0 / 32000.0))


def kernel(
    ab_sizes, cd_sizes, pairs_ref, amps_ref, ints_ref, out_ref,
    amps, ints, prod, from_core, x_one, x_two, from_y, cd_lab,
    x_one_out, x_two_out, y_out, targets,
    g_send, g_recv, r_send, r_recv, local_sem,
):
    panel_rows, depth = amps_ref.shape
    ab_rows = ints_ref.shape[0]
    rounds = panel_rows // CHUNK
    lane_tiles = depth // LANES
    round_rows = PANELS * CHUNK

    ab, cd = lax.axis_index("ab"), lax.axis_index("cd")
    yl, z = ab // 4, lax.rem(ab, 4)
    x, yh, core = cd // 4, lax.rem(cd // 2, 2), lax.rem(cd, 2)
    z_up, z_down, z_far = lax.rem(z + 1, 4), lax.rem(z + 3, 4), lax.rem(z + 2, 4)
    mine, other = yl * 4, (1 - yl) * 4

    to_pair = {"ab": other + z, "cd": cd}
    to_up = {"ab": mine + z_up, "cd": cd}
    to_down = {"ab": mine + z_down, "cd": cd}
    to_core = {"ab": ab, "cd": x * 4 + yh * 2 + (1 - core)}
    to_y = {"ab": ab, "cd": x * 4 + (1 - yh) * 2 + core}
    to_right = {"ab": ab, "cd": lax.rem(x + 1, 4) * 4 + yh * 2 + core}
    to_left = {"ab": ab, "cd": lax.rem(x + 3, 4) * 4 + yh * 2 + core}

    def ints_copy(block):
        k, dc, dy = block // 4, 1 - (block // 2) % 2, block % 2
        dx = 2 + 3 * k - k * (k - 1) // 2
        part = lax.rem(x + dx, 4) * 4 + (yh + dy - 2 * yh * dy) * 2 + (core + dc - 2 * core * dc)
        start = pl.multiple_of(part * LANES, LANES)
        copy = pltpu.make_async_copy(
            ints_ref.at[pl.ds(start, LANES), :],
            ints.at[pl.ds(pl.multiple_of(block * LANES, LANES), LANES), :],
            local_sem.at[block],
        )
        return copy, start

    blocks = ab_rows // LANES

    @pl.loop(0, blocks)
    def _(block):
        ints_copy(block)[0].start()

    barrier = pltpu.get_barrier_semaphore()
    neighbours = (to_pair, to_up, to_down, to_core, to_y, to_right, to_left)
    for neighbour in neighbours:
        pl.semaphore_signal(barrier, inc=1, device_id=neighbour, device_id_type=MESH)
    pl.semaphore_wait(barrier, len(neighbours))

    def slot(q, owner, low, high):
        start = pl.multiple_of(q * round_rows + owner * CHUNK, CHUNK)
        return amps.at[pl.ds(start, CHUNK), pl.ds(low * LANES, (high - low) * LANES)]

    full, cross, rest = (0, lane_tiles), (0, CROSS), (CROSS, lane_tiles)
    low_cut, high_cut = (0, CUT), (CUT, lane_tiles)
    low_rest, high_rest = (CROSS, CUT_REST), (CUT_REST, lane_tiles)
    me, up, down, far = mine + z, mine + z_up, mine + z_down, mine + z_far
    o_me, o_up, o_down, o_far = other + z, other + z_up, other + z_down, other + z_far
    kinds = (
        (me, full, to_pair, o_me),
        (me, full, to_up, down),
        (me, full, to_down, up),
        (o_me, rest, to_up, o_down),
        (o_me, rest, to_down, o_up),
        (down, low_cut, to_up, far),
        (up, high_cut, to_down, far),
        (down, cross, to_pair, o_down),
        (up, cross, to_pair, o_up),
        (o_down, low_rest, to_up, o_far),
        (o_up, high_rest, to_down, o_far),
        (far, cross, to_pair, o_far),
    )

    def g_out(q, kind):
        owner, columns, target, _ = kinds[kind]
        ref = slot(q, owner, *columns)
        own = amps_ref.at[pl.ds(pl.multiple_of(q * CHUNK, CHUNK), CHUNK), :]
        return pltpu.make_async_remote_copy(
            src_ref=own if kind < 3 else ref, dst_ref=ref,
            send_sem=g_send.at[kind, q], recv_sem=g_recv.at[kind, q],
            device_id=target, device_id_type=MESH,
        )

    def g_in(q, kind):
        _, columns, target, owner = kinds[kind]
        ref = slot(q, owner, *columns)
        return pltpu.make_async_remote_copy(
            src_ref=ref, dst_ref=ref, send_sem=g_send.at[kind, q], recv_sem=g_recv.at[kind, q],
            device_id=target, device_id_type=MESH,
        )

    def first(q):
        for kind in (1, 2, 0):
            g_out(q, kind).start()

    def second(q):
        g_in(q, 1).wait_recv()
        g_out(q, 5).start()
        g_out(q, 7).start()
        g_in(q, 2).wait_recv()
        g_out(q, 6).start()
        g_out(q, 8).start()
        g_in(q, 0).wait_recv()
        g_out(q, 3).start()
        g_out(q, 4).start()

    def third(q):
        g_in(q, 5).wait_recv()
        g_out(q, 11).start()
        g_in(q, 3).wait_recv()
        g_out(q, 9).start()
        g_in(q, 4).wait_recv()
        g_out(q, 10).start()

    def arrived(q):
        own_copy(q).wait()
        for kind in (6, 7, 8, 9, 10, 11):
            g_in(q, kind).wait_recv()

    def own_copy(q):
        return pltpu.make_async_copy(
            amps_ref.at[pl.ds(pl.multiple_of(q * CHUNK, CHUNK), CHUNK), :],
            slot(q, me, *full),
            local_sem.at[blocks + q],
        )

    first(0)
    first(1)

    @pl.loop(0, rounds)
    def _(q):
        own_copy(q).start()

    def ends(sizes):
        out, total = [], jnp.int32(0)
        for k in range(sizes.shape[0]):
            total = total + sizes[k]
            out.append(total)
        return out

    def labels(where_at, limits):
        label = jnp.zeros(where_at.shape, I32)
        for limit in limits:
            label = label + (where_at >= limit).astype(I32)
        return label.astype(F32).astype(BF16)

    ab_ends, cd_ends = ends(ab_sizes), ends(cd_sizes)
    cd_lab[...] = labels(cd * depth + lax.broadcasted_iota(I32, cd_lab.shape, 1), cd_ends)

    def mask(block):
        copy, start = ints_copy(block)
        copy.wait()
        at = lax.broadcasted_iota(I32, (LANES, LANES), 0) + (ab * ab_rows + start)
        ab_lab = labels(at, ab_ends)

        def one(k, carry):
            columns = pl.ds(pl.multiple_of(k * LANES, LANES), LANES)
            rows = pl.ds(pl.multiple_of(block * LANES, LANES), LANES)
            here = jnp.broadcast_to(cd_lab[0:1, columns], (LANES, LANES))
            tile = ints[rows, columns]
            ints[rows, columns] = jnp.where(ab_lab == here, tile, jnp.zeros_like(tile))
            return carry

        lax.fori_loop(0, lane_tiles, one, 0, unroll=5)

    wide = 4 * LANES
    half = 2 * LANES

    def r_copy(g, kind, src, dst, target):
        return pltpu.make_async_remote_copy(
            src_ref=src, dst_ref=dst, send_sem=r_send.at[kind, g], recv_sem=r_recv.at[kind, g],
            device_id=target, device_id_type=MESH,
        )

    def core_copy(g, k):
        src = prod.at[g, pl.ds(pl.multiple_of(k * wide, wide), half), :]
        dst = from_core.at[g, pl.ds(pl.multiple_of(k * half, half), half), :]
        return r_copy(g, k, src, dst, to_core)

    def x_one_copy(g, way):
        return r_copy(g, 4 + way, x_one_out.at[way, g], x_one.at[way, g], (to_right, to_left)[way])

    def x_two_copy(g, way):
        return r_copy(g, 6 + way, x_two_out.at[way, g], x_two.at[way, g], (to_right, to_left)[way])

    def y_copy(g):
        return r_copy(g, 8, y_out.at[g], from_y.at[g], to_y)

    def kept(k):
        return pl.ds(k * wide + half, half)

    def product(g, part, count):
        columns = pl.ds(pl.multiple_of(part * 2 * wide, 2 * wide), 2 * wide)
        rows = pl.ds(pl.multiple_of(g * round_rows, round_rows), count * round_rows)
        found = lax.dot_general(
            ints[columns, :], amps[rows, :], (((1,), (1,)), ((), ())), preferred_element_type=F32
        )
        for one in range(count):
            prod[g + one, columns, :] = found[:, one * round_rows : (one + 1) * round_rows]
        for k in range(2):
            for one in range(count):
                core_copy(g + one, 2 * part + k).start()

    def x_first(g):
        core_copy(g, 0).wait_recv()
        for way in range(2):
            at = half + way * LANES
            part = prod[g, pl.ds(at, LANES), :] + from_core[g, pl.ds(way * LANES, LANES), :]
            x_one_out[way, g] = encode(part)
            x_one_copy(g, way).start()

    def x_second(g):
        for way in range(2):
            core_copy(g, 1 + way).wait_recv()
            part = prod[g, kept(1 + way), :] + from_core[g, pl.ds((1 + way) * half, half), :]
            x_one_copy(g, way).wait_recv()
            more = decode(x_one[way, g])
            low, high = part[:LANES], part[LANES:]
            low, high = (low, high + more) if way else (low + more, high)
            x_two_out[way, g] = encode(jnp.concatenate([low, high], axis=0))
            x_two_copy(g, way).start()

    def y_step(g):
        core_copy(g, 3).wait_recv()
        total = prod[g, kept(3), :] + from_core[g, pl.ds(3 * half, half), :]
        x_two_copy(g, 0).wait_recv()
        x_two_copy(g, 1).wait_recv()
        total = total + decode(x_two[0, g]) + decode(x_two[1, g])
        y_out[g] = encode(total[LANES:])
        y_copy(g).start()
        prod[g, pl.ds(3 * wide + half, LANES), :] = total[:LANES]

    def place(g):
        shape = (out_ref.shape[0], round_rows)
        target = jnp.broadcast_to(targets[pl.ds(g, 1), :], shape)
        goes = lax.broadcasted_iota(I32, shape, 0) == target
        goes = jnp.where(goes, 1.0, 0.0).astype(BF16)
        y_copy(g).wait_recv()
        found = prod[g, pl.ds(3 * wide + half, LANES), :] + decode(from_y[g])
        high = found.astype(BF16)
        left = found - high.astype(F32)
        mid = left.astype(BF16)
        low = (left - mid.astype(F32)).astype(BF16)
        term = lax.dot_general(
            jnp.concatenate([goes, goes, goes], axis=1), jnp.concatenate([high, mid, low], axis=1),
            (((1,), (1,)), ((), ())), preferred_element_type=F32,
        )
        out_ref[...] += term
        for kind in range(len(kinds)):
            g_out(g, kind).wait_send()
        for k in range(4):
            core_copy(g, k).wait_send()
        for way in range(2):
            x_one_copy(g, way).wait_send()
            x_two_copy(g, way).wait_send()
        y_copy(g).wait_send()

    pairs = pairs_ref[...]
    chunk = lax.broadcasted_iota(I32, pairs.shape, 1) // CHUNK
    panel = lax.broadcasted_iota(I32, pairs.shape, 0)
    turned = [pairs if m == 0 else pltpu.roll(pairs, m * CHUNK, 1) for m in range(rounds)]
    for g in range(rounds):
        chosen = jnp.zeros_like(pairs)
        for p in range(PANELS):
            chosen = jnp.where((panel == p) & (chunk == p), turned[(p - g) % rounds], chosen)
        targets[g : g + 1, :] = jnp.sum(chosen, axis=0, keepdims=True)

    def in_range(step, n):
        pl.when((n >= 0) & (n < rounds))(lambda: step(n))

    late = rounds - LATE

    def together(step, n):
        @pl.when((n >= 0) & (n < rounds) & ((n >= late) | (n % 2 == 1)))
        def _():
            pl.loop(n - (n < late).astype(I32), n + 1)(step)

    does = {
        "first": functools.partial(in_range, first),
        "second": functools.partial(in_range, second),
        "third": functools.partial(in_range, third),
        "arrived": functools.partial(in_range, arrived),
        "x one": functools.partial(together, x_first),
        "x two": functools.partial(together, x_second),
        "y": functools.partial(together, y_step),
        "place": functools.partial(together, place),
    }
    out_ref[...] = jnp.zeros_like(out_ref)

    @pl.loop(0, 2 * (rounds + DRAIN))
    def _(h):
        q = h // 2

        for parity in range(2):

            @pl.when(h % 2 == parity)
            def _():
                for name, lag in STAGES[parity]:
                    does[name](q - lag)

        @pl.when(h < blocks // 4)
        def _():
            @pl.loop(0, 4)
            def _(block):
                mask(4 * h + block)

        ready, part = (h + 8 - MULTIPLY) // 2 - 4, (h + 8 - MULTIPLY) % 2

        @pl.when((ready >= late) & (ready < rounds))
        def _():
            product(ready, part, 1)

        @pl.when((ready >= 0) & (ready < late) & (ready % 2 == 1))
        def _():
            product(ready - 1, part, 2)


def shards(amplitudes, integrals, ab_sizes, cd_sizes, pair_index):
    panel_rows, depth = amplitudes.shape
    ab_rows = integrals.shape[0]
    all_pairs = pair_index.shape[0]
    rounds = panel_rows // CHUNK
    keeps = ab_rows // lax.axis_size("cd")
    pairs = pair_index.reshape(PANELS, panel_rows)
    sums = (
        pltpu.VMEM((2, rounds, keeps + CHUNK, PANELS * CHUNK), jnp.int16),
        pltpu.VMEM((2, rounds, 2 * keeps + CHUNK, PANELS * CHUNK), jnp.int16),
        pltpu.VMEM((rounds, keeps + CHUNK, PANELS * CHUNK), jnp.int16),
    )
    vmem, smem = pl.BlockSpec(memory_space=pltpu.VMEM), pl.BlockSpec(memory_space=pltpu.SMEM)
    hbm = pl.BlockSpec(memory_space=pl.ANY)
    return pl.pallas_call(
        kernel,
        out_shape=pltpu.VMEM((all_pairs, keeps), F32),
        in_specs=[smem, smem, vmem, hbm, hbm],
        out_specs=vmem,
        scratch_shapes=[
            pltpu.VMEM((all_pairs, depth), BF16),
            pltpu.VMEM((ab_rows, depth), BF16),
            pltpu.VMEM((rounds, ab_rows, PANELS * CHUNK), F32),
            pltpu.VMEM((rounds, ab_rows // 2, PANELS * CHUNK), F32),
            *sums,
            pltpu.VMEM((16, depth), BF16),
            *sums,
            pltpu.VMEM((rounds, PANELS * CHUNK), I32),
            pltpu.SemaphoreType.DMA((12, rounds)),
            pltpu.SemaphoreType.DMA((12, rounds)),
            pltpu.SemaphoreType.DMA((9, rounds)),
            pltpu.SemaphoreType.DMA((9, rounds)),
            pltpu.SemaphoreType.DMA((ab_rows // LANES + rounds,)),
        ],
        name="ladder",
        compiler_params=pltpu.CompilerParams(
            collective_id=0, has_side_effects=True, vmem_limit_bytes=56 << 20
        ),
    )(ab_sizes, cd_sizes, pairs, amplitudes, integrals)


def solution(mesh):
    return jax.shard_map(
        shards,
        mesh=mesh,
        in_specs=(P("ab", "cd"), P("ab", "cd"), P(), P(), P()),
        out_specs=P(None, ("ab", "cd")),
        check_vma=False,
    )
```

```python
import functools

import jax
import jax.numpy as jnp
from jax import lax
from jax.experimental import pallas as pl
from jax.experimental.pallas import tpu as pltpu
from jax.sharding import PartitionSpec as P

MESH = pl.DeviceIdType.MESH
BF16, F32, I32 = jnp.bfloat16, jnp.float32, jnp.int32

PANELS = 8
LANES = 128
CHUNK = 16

CROSS = 10
CUT = 13
CUT_REST = 17

STAGES = (
    (("third", 1), ("second", 0), ("first", -2), ("y", 6), ("x one", 2)),
    (("arrived", 1), ("x two", 3), ("place", 8)),
)
MULTIPLY = 3
DRAIN = 8
LATE = 2

def encode(values):
    largest = jnp.maximum(jnp.max(jnp.abs(values), axis=0, keepdims=True), 1e-30)
    size = jnp.ceil(jnp.log2(largest) * 16.0) + 1.0
    codes = jnp.round(values * (jnp.exp2(size * -0.0625) * 32000.0)).astype(I32)
    sizes = jnp.broadcast_to(size, (CHUNK, values.shape[1])).astype(I32)
    return jnp.concatenate([codes, sizes], axis=0).astype(jnp.int16)


def decode(codes):
    codes = codes.astype(I32).astype(F32)
    rows = codes.shape[0] - CHUNK
    return codes[:rows] * (jnp.exp2(codes[rows : rows + 1] * 0.0625) * (1.0 / 32000.0))


def kernel(
    ab_sizes, cd_sizes, pairs_ref, amps_ref, ints_ref, out_ref,
    amps, ints, prod, from_core, x_one, x_two, from_y, cd_lab,
    x_one_out, x_two_out, y_out, targets,
    g_send, g_recv, r_send, r_recv, local_sem,
):
    panel_rows, depth = amps_ref.shape
    ab_rows = ints_ref.shape[0]
    rounds = panel_rows // CHUNK
    lane_tiles = depth // LANES
    round_rows = PANELS * CHUNK

    ab, cd = lax.axis_index("ab"), lax.axis_index("cd")
    yl, z = ab // 4, lax.rem(ab, 4)
    x, yh, core = cd // 4, lax.rem(cd // 2, 2), lax.rem(cd, 2)
    z_up, z_down, z_far = lax.rem(z + 1, 4), lax.rem(z + 3, 4), lax.rem(z + 2, 4)
    mine, other = yl * 4, (1 - yl) * 4

    to_pair = {"ab": other + z, "cd": cd}
    to_up = {"ab": mine + z_up, "cd": cd}
    to_down = {"ab": mine + z_down, "cd": cd}
    to_core = {"ab": ab, "cd": x * 4 + yh * 2 + (1 - core)}
    to_y = {"ab": ab, "cd": x * 4 + (1 - yh) * 2 + core}
    to_right = {"ab": ab, "cd": lax.rem(x + 1, 4) * 4 + yh * 2 + core}
    to_left = {"ab": ab, "cd": lax.rem(x + 3, 4) * 4 + yh * 2 + core}

    barrier = pltpu.get_barrier_semaphore()
    neighbours = (to_pair, to_up, to_down, to_core, to_y, to_right, to_left)
    for neighbour in neighbours:
        pl.semaphore_signal(barrier, inc=1, device_id=neighbour, device_id_type=MESH)

    def ints_copy(block):
        k, dc, dy = block // 4, 1 - (block // 2) % 2, block % 2
        dx = 2 + 3 * k - k * (k - 1) // 2
        part = lax.rem(x + dx, 4) * 4 + (yh + dy - 2 * yh * dy) * 2 + (core + dc - 2 * core * dc)
        start = pl.multiple_of(part * LANES, LANES)
        copy = pltpu.make_async_copy(
            ints_ref.at[pl.ds(start, LANES), :],
            ints.at[pl.ds(pl.multiple_of(block * LANES, LANES), LANES), :],
            local_sem.at[block],
        )
        return copy, start

    blocks = ab_rows // LANES

    @pl.loop(0, blocks)
    def _(block):
        ints_copy(block)[0].start()

    pl.semaphore_wait(barrier, len(neighbours))

    def slot(q, owner, low, high):
        start = pl.multiple_of(q * round_rows + owner * CHUNK, CHUNK)
        return amps.at[pl.ds(start, CHUNK), pl.ds(low * LANES, (high - low) * LANES)]

    full, cross, rest = (0, lane_tiles), (0, CROSS), (CROSS, lane_tiles)
    low_cut, high_cut = (0, CUT), (CUT, lane_tiles)
    low_rest, high_rest = (CROSS, CUT_REST), (CUT_REST, lane_tiles)
    me, up, down, far = mine + z, mine + z_up, mine + z_down, mine + z_far
    o_me, o_up, o_down, o_far = other + z, other + z_up, other + z_down, other + z_far
    kinds = (
        (me, full, to_pair, o_me),
        (me, full, to_up, down),
        (me, full, to_down, up),
        (o_me, rest, to_up, o_down),
        (o_me, rest, to_down, o_up),
        (down, low_cut, to_up, far),
        (up, high_cut, to_down, far),
        (down, cross, to_pair, o_down),
        (up, cross, to_pair, o_up),
        (o_down, low_rest, to_up, o_far),
        (o_up, high_rest, to_down, o_far),
        (far, cross, to_pair, o_far),
    )

    def g_out(q, kind):
        owner, columns, target, _ = kinds[kind]
        ref = slot(q, owner, *columns)
        own = amps_ref.at[pl.ds(pl.multiple_of(q * CHUNK, CHUNK), CHUNK), :]
        return pltpu.make_async_remote_copy(
            src_ref=own if kind < 3 else ref, dst_ref=ref,
            send_sem=g_send.at[kind, q], recv_sem=g_recv.at[kind, q],
            device_id=target, device_id_type=MESH,
        )

    def g_in(q, kind):
        _, columns, target, owner = kinds[kind]
        ref = slot(q, owner, *columns)
        return pltpu.make_async_remote_copy(
            src_ref=ref, dst_ref=ref, send_sem=g_send.at[kind, q], recv_sem=g_recv.at[kind, q],
            device_id=target, device_id_type=MESH,
        )

    def first(q):
        for kind in (1, 2, 0):
            g_out(q, kind).start()

    def second(q):
        g_in(q, 1).wait_recv()
        g_out(q, 5).start()
        g_out(q, 7).start()
        g_in(q, 2).wait_recv()
        g_out(q, 6).start()
        g_out(q, 8).start()
        g_in(q, 0).wait_recv()
        g_out(q, 3).start()
        g_out(q, 4).start()

    def third(q):
        g_in(q, 5).wait_recv()
        g_out(q, 11).start()
        g_in(q, 3).wait_recv()
        g_out(q, 9).start()
        g_in(q, 4).wait_recv()
        g_out(q, 10).start()

    def arrived(q):
        own_copy(q).wait()
        for kind in (6, 7, 8, 9, 10, 11):
            g_in(q, kind).wait_recv()

    def own_copy(q):
        return pltpu.make_async_copy(
            amps_ref.at[pl.ds(pl.multiple_of(q * CHUNK, CHUNK), CHUNK), :],
            slot(q, me, *full),
            local_sem.at[blocks + q],
        )

    first(0)
    first(1)

    @pl.loop(0, rounds)
    def _(q):
        own_copy(q).start()

    def ends(sizes):
        out, total = [], jnp.int32(0)
        for k in range(sizes.shape[0]):
            total = total + sizes[k]
            out.append(total)
        return out

    def labels(where_at, limits):
        label = jnp.zeros(where_at.shape, I32)
        for limit in limits:
            label = label + (where_at >= limit).astype(I32)
        return label.astype(F32).astype(BF16)

    ab_ends, cd_ends = ends(ab_sizes), ends(cd_sizes)
    cd_lab[...] = labels(cd * depth + lax.broadcasted_iota(I32, cd_lab.shape, 1), cd_ends)

    def mask(block):
        copy, start = ints_copy(block)
        copy.wait()
        at = lax.broadcasted_iota(I32, (LANES, LANES), 0) + (ab * ab_rows + start)
        ab_lab = labels(at, ab_ends)

        def one(k, carry):
            columns = pl.ds(pl.multiple_of(k * LANES, LANES), LANES)
            rows = pl.ds(pl.multiple_of(block * LANES, LANES), LANES)
            here = jnp.broadcast_to(cd_lab[0:1, columns], (LANES, LANES))
            tile = ints[rows, columns]
            ints[rows, columns] = jnp.where(ab_lab == here, tile, jnp.zeros_like(tile))
            return carry

        lax.fori_loop(0, lane_tiles, one, 0, unroll=5)

    wide = 4 * LANES
    half = 2 * LANES

    def r_copy(g, kind, src, dst, target):
        return pltpu.make_async_remote_copy(
            src_ref=src, dst_ref=dst, send_sem=r_send.at[kind, g], recv_sem=r_recv.at[kind, g],
            device_id=target, device_id_type=MESH,
        )

    def core_copy(g, k):
        src = prod.at[g, pl.ds(pl.multiple_of(k * wide, wide), half), :]
        dst = from_core.at[g, pl.ds(pl.multiple_of(k * half, half), half), :]
        return r_copy(g, k, src, dst, to_core)

    def x_one_copy(g, way):
        return r_copy(g, 4 + way, x_one_out.at[way, g], x_one.at[way, g], (to_right, to_left)[way])

    def x_two_copy(g, way):
        return r_copy(g, 6 + way, x_two_out.at[way, g], x_two.at[way, g], (to_right, to_left)[way])

    def y_copy(g):
        return r_copy(g, 8, y_out.at[g], from_y.at[g], to_y)

    def kept(k):
        return pl.ds(k * wide + half, half)

    def product(g, part, count):
        columns = pl.ds(pl.multiple_of(part * 2 * wide, 2 * wide), 2 * wide)
        rows = pl.ds(pl.multiple_of(g * round_rows, round_rows), count * round_rows)
        found = lax.dot_general(
            ints[columns, :], amps[rows, :], (((1,), (1,)), ((), ())), preferred_element_type=F32
        )
        for one in range(count):
            prod[g + one, columns, :] = found[:, one * round_rows : (one + 1) * round_rows]
        for k in range(2):
            for one in range(count):
                core_copy(g + one, 2 * part + k).start()

    def x_first(g):
        core_copy(g, 0).wait_recv()
        for way in range(2):
            at = half + way * LANES
            part = prod[g, pl.ds(at, LANES), :] + from_core[g, pl.ds(way * LANES, LANES), :]
            x_one_out[way, g] = encode(part)
            x_one_copy(g, way).start()

    def x_second(g):
        for way in range(2):
            core_copy(g, 1 + way).wait_recv()
            part = prod[g, kept(1 + way), :] + from_core[g, pl.ds((1 + way) * half, half), :]
            x_one_copy(g, way).wait_recv()
            more = decode(x_one[way, g])
            low, high = part[:LANES], part[LANES:]
            low, high = (low, high + more) if way else (low + more, high)
            x_two_out[way, g] = encode(jnp.concatenate([low, high], axis=0))
            x_two_copy(g, way).start()

    def y_step(g):
        core_copy(g, 3).wait_recv()
        total = prod[g, kept(3), :] + from_core[g, pl.ds(3 * half, half), :]
        x_two_copy(g, 0).wait_recv()
        x_two_copy(g, 1).wait_recv()
        total = total + decode(x_two[0, g]) + decode(x_two[1, g])
        y_out[g] = encode(total[LANES:])
        y_copy(g).start()
        prod[g, pl.ds(3 * wide + half, LANES), :] = total[:LANES]

    def place(g):
        shape = (out_ref.shape[0], round_rows)
        target = jnp.broadcast_to(targets[pl.ds(g, 1), :], shape)
        goes = lax.broadcasted_iota(I32, shape, 0) == target
        goes = jnp.where(goes, 1.0, 0.0).astype(BF16)
        y_copy(g).wait_recv()
        found = prod[g, pl.ds(3 * wide + half, LANES), :] + decode(from_y[g])
        high = found.astype(BF16)
        left = found - high.astype(F32)
        mid = left.astype(BF16)
        low = (left - mid.astype(F32)).astype(BF16)
        term = lax.dot_general(
            jnp.concatenate([goes, goes, goes], axis=1), jnp.concatenate([high, mid, low], axis=1),
            (((1,), (1,)), ((), ())), preferred_element_type=F32,
        )
        out_ref[...] += term
        for kind in range(len(kinds)):
            g_out(g, kind).wait_send()
        for k in range(4):
            core_copy(g, k).wait_send()
        for way in range(2):
            x_one_copy(g, way).wait_send()
            x_two_copy(g, way).wait_send()
        y_copy(g).wait_send()

    pairs = pairs_ref[...]
    chunk = lax.broadcasted_iota(I32, pairs.shape, 1) // CHUNK
    panel = lax.broadcasted_iota(I32, pairs.shape, 0)
    turned = [pairs if m == 0 else pltpu.roll(pairs, m * CHUNK, 1) for m in range(rounds)]
    for g in range(rounds):
        chosen = jnp.zeros_like(pairs)
        for p in range(PANELS):
            chosen = jnp.where((panel == p) & (chunk == p), turned[(p - g) % rounds], chosen)
        targets[g : g + 1, :] = jnp.sum(chosen, axis=0, keepdims=True)

    def in_range(step, n):
        pl.when((n >= 0) & (n < rounds))(lambda: step(n))

    late = rounds - LATE

    def together(step, n):
        @pl.when((n >= 0) & (n < rounds) & ((n >= late) | (n % 2 == 1)))
        def _():
            pl.loop(n - (n < late).astype(I32), n + 1)(step)

    does = {
        "first": functools.partial(in_range, first),
        "second": functools.partial(in_range, second),
        "third": functools.partial(in_range, third),
        "arrived": functools.partial(in_range, arrived),
        "x one": functools.partial(together, x_first),
        "x two": functools.partial(together, x_second),
        "y": functools.partial(together, y_step),
        "place": functools.partial(together, place),
    }
    out_ref[...] = jnp.zeros_like(out_ref)

    @pl.loop(0, 2 * (rounds + DRAIN))
    def _(h):
        q = h // 2

        for parity in range(2):

            @pl.when(h % 2 == parity)
            def _():
                for name, lag in STAGES[parity]:
                    does[name](q - lag)

        @pl.when(h < blocks // 4)
        def _():
            @pl.loop(0, 4)
            def _(block):
                mask(4 * h + block)

        ready, part = (h + 8 - MULTIPLY) // 2 - 4, (h + 8 - MULTIPLY) % 2

        @pl.when((ready >= late) & (ready < rounds))
        def _():
            product(ready, part, 1)

        @pl.when((ready >= 0) & (ready < late) & (ready % 2 == 1))
        def _():
            product(ready - 1, part, 2)


def shards(amplitudes, integrals, ab_sizes, cd_sizes, pair_index):
    panel_rows, depth = amplitudes.shape
    ab_rows = integrals.shape[0]
    all_pairs = pair_index.shape[0]
    rounds = panel_rows // CHUNK
    keeps = ab_rows // lax.axis_size("cd")
    pairs = pair_index.reshape(PANELS, panel_rows)
    sums = (
        pltpu.VMEM((2, rounds, keeps + CHUNK, PANELS * CHUNK), jnp.int16),
        pltpu.VMEM((2, rounds, 2 * keeps + CHUNK, PANELS * CHUNK), jnp.int16),
        pltpu.VMEM((rounds, keeps + CHUNK, PANELS * CHUNK), jnp.int16),
    )
    vmem, smem = pl.BlockSpec(memory_space=pltpu.VMEM), pl.BlockSpec(memory_space=pltpu.SMEM)
    hbm = pl.BlockSpec(memory_space=pl.ANY)
    return pl.pallas_call(
        kernel,
        out_shape=pltpu.VMEM((all_pairs, keeps), F32),
        in_specs=[smem, smem, vmem, hbm, hbm],
        out_specs=vmem,
        scratch_shapes=[
            pltpu.VMEM((all_pairs, depth), BF16),
            pltpu.VMEM((ab_rows, depth), BF16),
            pltpu.VMEM((rounds, ab_rows, PANELS * CHUNK), F32),
            pltpu.VMEM((rounds, ab_rows // 2, PANELS * CHUNK), F32),
            *sums,
            pltpu.VMEM((16, depth), BF16),
            *sums,
            pltpu.VMEM((rounds, PANELS * CHUNK), I32),
            pltpu.SemaphoreType.DMA((12, rounds)),
            pltpu.SemaphoreType.DMA((12, rounds)),
            pltpu.SemaphoreType.DMA((9, rounds)),
            pltpu.SemaphoreType.DMA((9, rounds)),
            pltpu.SemaphoreType.DMA((ab_rows // LANES + rounds,)),
        ],
        name="ladder",
        compiler_params=pltpu.CompilerParams(
            collective_id=0, has_side_effects=True, vmem_limit_bytes=56 << 20
        ),
    )(ab_sizes, cd_sizes, pairs, amplitudes, integrals)


def solution(mesh):
    return jax.shard_map(
        shards,
        mesh=mesh,
        in_specs=(P("ab", "cd"), P("ab", "cd"), P(), P(), P()),
        out_specs=P(None, ("ab", "cd")),
        check_vma=False,
    )
```
